256 devices in a mesh: rows: 32 (over y_lo, z, core), mz: 8 (over x, y_hi).
Axes of the slice: x: 4, y: 4 (y_hi: 2, y_lo: 2; y = y_hi * 2 + y_lo), z: 8, core: 2. Of those that a mesh axis runs over, the one named last changes fastest.
Arguments:
- raw_scans: float32 [12288, 49152], P('rows', 'mz'), may hold values from 0.02 to 4
- scan_shift: int32 [12288], P('rows'), may hold values from -16 to 15, as said below
- scan_weight: int32 [12288], P('rows'), may hold values from 0 to 255
- spectra_init: float32 [64, 49152], P(None, 'mz'), may hold values from 0.05 to 1
Outputs:
- concentrations: float32 [12288, 64], P('rows')
- spectra: float32 [64, 49152], P(None, 'mz')
The draws below stay inside these ranges and needn't reach their ends.
Inputs may be any that keep to these rules, and one draw needn't show every extreme that they name: `scan_shift`: every aligned scan reads two raw scans of its own run; the first run holds 3088 scans, the last 3056, the others 12288 // 4; the offsets follow piecewise linear warps over segments of 32 rows counted from each run's start.
All inputs are finite; a program needn't handle non-finite values.
Results may differ from the reference program's by a relative error of at most 0.0003.
Values sent between devices are 32-bit elements; how exact they have to be, the bound alone decides.
A program may use at most 128 MiB of HBM per device.

```python
import math
import jax
import jax.numpy as jnp
from jax import lax

MZ = 49152
K = 64
ROWS_DEV = 384
RUNS = 4
SEG = 32
HALO = 16
SWEEPS = 2
ROWS = 12288


def warp_tables(key):
    quarter = ROWS // RUNS
    half_seg = SEG // 2
    run_ids = jnp.arange(RUNS, dtype=jnp.int32)
    starts = run_ids * quarter + jnp.where(run_ids > 0, half_seg, 0).astype(jnp.int32)
    ends = jnp.concatenate([starts[1:], jnp.array([ROWS], jnp.int32)])
    lengths = ends - starts
    global_row = jnp.arange(ROWS, dtype=jnp.int32)
    run_of = jnp.sum((global_row[:, None] >= starts[None, 1:]).astype(jnp.int32), axis=1)
    within = global_row - starts[run_of]
    knot_count = (quarter + half_seg) // SEG + 2
    knot_values = jax.random.randint(jax.random.fold_in(key, 17), (RUNS, knot_count), -HALO * 256, (HALO - 1) * 256 + 1)
    knot_values = knot_values.at[:, 1].set(-HALO * 256)
    knot_values = knot_values.at[:, 2].set((HALO - 1) * 256)
    knot_values = knot_values.at[:, 3].set((HALO - 1) * 256 - 1)
    lower_seg = (quarter - half_seg) // SEG
    crossing = (HALO - 1) * 256
    knot_values = knot_values.at[1, lower_seg].set(crossing)
    knot_values = knot_values.at[1, lower_seg + 1].set(-crossing - 2)
    upper_seg = (ROWS_DEV - 1 - half_seg) // SEG
    knot_values = knot_values.at[2, upper_seg].set((HALO - 1) * 256)
    knot_values = knot_values.at[2, upper_seg + 1].set((HALO - 1) * 256)
    segment_index = within // SEG
    position = within % SEG
    start_vals = knot_values[run_of, segment_index]
    end_vals = knot_values[run_of, segment_index + 1]
    fixed_point = start_vals + (end_vals - start_vals) * position // SEG
    integer_part = fixed_point // 256
    fraction_part = fixed_point - integer_part * 256
    source_row = jnp.clip(within + integer_part, 0, lengths[run_of] - 2)
    offsets = source_row - within
    return (offsets.astype(jnp.int32), fraction_part.astype(jnp.int32))


def draw_scan_shift(key, part):
    return warp_tables(key)[0]


def draw_scan_weight(key, part):
    return warp_tables(key)[1]


def block_levels(rng, shape, split, smallest, high):
    factor_of = 1.0
    for dim, shards_of in split:
        draws = jax.random.uniform(jax.random.fold_in(jax.random.fold_in(rng, 6), dim), (shards_of,), jnp.float32, smallest / len(split), high / len(split))
        factor_of = factor_of * jnp.repeat(jnp.exp(draws), shape[dim] // shards_of).reshape((-1,) + (1,) * (len(shape) - 1 - dim))
    return factor_of


def setup_inputs(seed: int = 0) -> dict:
    key_list = jax.random.split(jax.random.key(seed), 5)
    return {
        "raw_scans": jnp.clip(jnp.exp(math.log(4.0) - 5.2983174 * jax.random.uniform(key_list[0], (ROWS, MZ), jnp.float32) ** block_levels(key_list[0], (ROWS, MZ), ((0, 32), (1, 8)), -0.2, 0.2)), 0.02, 4.0),
        "scan_shift": draw_scan_shift(jax.random.fold_in(key_list[4], 71), 0),
        "scan_weight": draw_scan_weight(jax.random.fold_in(key_list[4], 71), 0),
        "spectra_init": jnp.clip(0.05 + 0.95 * jax.random.uniform(key_list[3], (K, MZ), jnp.float32) ** block_levels(key_list[3], (K, MZ), ((1, 8),), -0.2, 0.2), 0.05, 1.0),
    }


fraction_unit = 256.0
rms_epsilon = 1e-06
ridge_share = 0.01

def dot_highest(left, right):
    return jnp.dot(left.astype(jnp.float32), right.astype(jnp.float32), precision=lax.Precision.HIGHEST, preferred_element_type=jnp.float32)

def ridge_solve(gram, target):
    width_count = gram.shape[0]
    ridge_level = ridge_share * jnp.trace(gram) / width_count
    factor = jnp.linalg.cholesky(gram + ridge_level * jnp.eye(width_count, dtype=jnp.float32))
    return jax.scipy.linalg.cho_solve((factor, True), target)

def reference(raw_scans, scan_shift, scan_weight, spectra_init):
    total_rows = raw_scans.shape[0]
    row_index = jnp.arange(total_rows, dtype=jnp.int32) + scan_shift
    fraction = scan_weight.astype(jnp.float32) / fraction_unit
    warped = raw_scans[row_index] * (1.0 - fraction)[:, None] + raw_scans[row_index + 1] * fraction[:, None]
    spectra = spectra_init
    spectra_gram = dot_highest(spectra, spectra.T)
    concentrations = jnp.zeros((total_rows, K), jnp.float32)
    for sweep_index in range(SWEEPS):
        scores = dot_highest(warped, spectra.T)
        concentrations = jnp.maximum(ridge_solve(spectra_gram, scores.T).T, 0.0)
        concentration_gram = dot_highest(concentrations.T, concentrations)
        cross = dot_highest(concentrations.T, warped)
        raw_spectra = jnp.maximum(ridge_solve(concentration_gram, cross), 0.0)
        squares = lax.optimization_barrier(jnp.sum(raw_spectra * raw_spectra, axis=1))
        scales = jnp.sqrt(squares / MZ + rms_epsilon)
        spectra = raw_spectra / scales[:, None]
        spectra_gram = dot_highest(spectra, spectra.T)
    return (concentrations, spectra)
```

```python
import functools

import jax
import jax.numpy as jnp
from jax import lax
from jax.experimental import pallas as pl
from jax.experimental.pallas import tpu as pltpu
from jax.sharding import PartitionSpec as P

MESH = pl.DeviceIdType.MESH
F32 = jnp.float32
BF16 = jnp.bfloat16

MZ = 49152
K = 64
HALO = 16
SWEEPS = 2
ROW_DEVS = 32
MZ_DEVS = 8
RING = 8
ROWS = 384
PADDED = ROWS + 2 * HALO
TALL = 512
COLS = 6144
BLOCK = COLS // RING
HALF = BLOCK // 2
TILE = 128

fraction_unit = 256.0
rms_epsilon = 1e-06
ridge_share = 0.01

ORDER = (4, 3, 5, 2, 6, 1, 7, 0)


def split(x):
    high = x.astype(BF16)
    return high, (x - high.astype(F32)).astype(BF16)


def dot(left, right, dims, precision=None):
    return lax.dot_general(
        left, right, (dims, ((), ())), precision=precision, preferred_element_type=F32
    )


NN = ((1,), (0,))
NT = ((1,), (1,))
TN = ((0,), (0,))
HIGHEST = lax.Precision.HIGHEST


def iota(shape, dim):
    return lax.broadcasted_iota(jnp.int32, shape, dim)


def pack_gram(gram):
    return jnp.concatenate([gram[: K // 2], gram[K // 2 :]], axis=1)


def unpack_gram(packed):
    return jnp.concatenate([packed[:, :K], packed[:, K:]], axis=0)


def factor_start(gram):
    eye = iota((K, K), 0) == iota((K, K), 1)
    diagonal = jnp.where(eye, gram, 0.0)
    trace = jnp.sum(jnp.sum(diagonal, axis=1, keepdims=True), axis=0, keepdims=True)
    ridge = ridge_share * trace / K
    unit = jnp.where(eye, 1.0, 0.0).astype(F32)
    joined = jnp.concatenate([gram + unit * ridge, unit], axis=1)
    return tuple(joined[8 * j : 8 * j + 8] for j in range(8))


def factor_steps(groups, first, last):
    sub = iota((8, 1), 0)

    def step(g, groups):
        groups = list(groups)
        for p in range(8):
            pivot = groups[0][p : p + 1, p : p + 1]
            inverse = lax.rsqrt(pivot)
            inverse = inverse * (1.5 - 0.5 * pivot * inverse * inverse)
            row = groups[0][p : p + 1, :] * inverse
            for j in range(1, 8):
                column = jnp.where(j < 8 - g, groups[j][:, p : p + 1] * inverse, 0.0)
                groups[j] = groups[j] - column * row
            column = jnp.where(sub > p, groups[0][:, p : p + 1] * inverse, 0.0)
            groups[0] = jnp.where(sub == p, row, groups[0] - column * row)
        rolled = [pltpu.roll(x, 2 * K - 8, 1) for x in groups]
        return tuple(rolled[1:] + rolled[:1])

    return lax.fori_loop(first, last, step, groups)


def factor_end(groups):
    return jnp.concatenate(groups, axis=0)[:, :K]


def solve(inverse_factor, target):
    return dot(inverse_factor, dot(inverse_factor, target, NN, HIGHEST), TN, HIGHEST)


def kernel(
    raw, shift, weight, spec, conc_out, spec_out,
    raw32, spec32, halo32, high, low, spec2, halo2, warp, acc, gram_acc,
    gram_send, gram_recv, score_send, score_recv, score_sum, score_all,
    conc_gram, conc_gram_core, conc_gram_pair, conc_gram_y, conc_gram_all,
    spread, spread2, cross, cross_core, chain_up, chain_down, cross_y,
    found, square_recv, load_sem, send_sem, recv_sem,
):
    ri = lax.axis_index("rows")
    mj = lax.axis_index("mz")
    core = lax.rem(ri, 2)
    z = lax.rem(lax.div(ri, 2), RING)
    plane = ri - 2 * z

    def at_z(distance):
        return lax.rem(z + distance, RING)

    def z_device(distance):
        return plane + 2 * at_z(distance)

    partner = ri + 1 - 2 * core
    y_pair = lax.rem(ri + 16, ROW_DEVS)
    row_next = lax.rem(ri + 1, ROW_DEVS)
    row_back = lax.rem(ri + ROW_DEVS - 1, ROW_DEVS)
    started = []

    def send(source, target, rows=None, mz=None):
        number = len(started)
        copy = pltpu.make_async_remote_copy(
            src_ref=source,
            dst_ref=target,
            send_sem=send_sem.at[number],
            recv_sem=recv_sem.at[number],
            device_id=(ri if rows is None else rows, mj if mz is None else mz),
            device_id_type=MESH,
        )
        copy.start()
        started.append(copy)
        return copy

    def block_columns(b):
        return pl.ds(pl.multiple_of(b * BLOCK, TILE), BLOCK)

    spec_load = pltpu.make_async_copy(spec, spec32, load_sem.at[RING])
    spec_load.start()
    loads = []
    for b in range(RING):
        columns = pl.ds(b * BLOCK, BLOCK)
        loads.append(pltpu.make_async_copy(raw.at[:, columns], raw32.at[:, columns], load_sem.at[b]))
        loads[-1].start()

    barrier = pltpu.get_barrier_semaphore()
    peers = [(ri, lax.rem(mj + d, MZ_DEVS)) for d in range(1, MZ_DEVS)]
    peers += [(z_device(d), mj) for d in range(1, RING)]
    peers += [(y_pair, mj), (row_next, mj), (row_back, mj)]
    for peer in peers:
        pl.semaphore_signal(barrier, inc=1, device_id=peer, device_id_type=MESH)

    for t in range(3):
        target = iota((2 * TILE, TILE), 1) + shift[:, t * TILE : (t + 1) * TILE] + HALO
        fraction = weight[:, t * TILE : (t + 1) * TILE].astype(F32) / fraction_unit
        row = iota((2 * TILE, TILE), 0)
        warp[t] = jnp.where(row == target, 1.0 - fraction, 0.0) + jnp.where(
            row == target + 1, fraction, 0.0
        )
    acc[...] = jnp.zeros_like(acc)
    gram_acc[...] = jnp.zeros_like(gram_acc)

    pl.semaphore_wait(barrier, len(peers))
    halo_up = send(raw.at[pl.ds(ROWS - HALO, HALO), :], halo32.at[0], rows=row_next)
    halo_down = send(raw.at[pl.ds(0, HALO), :], halo32.at[1], rows=row_back)

    def square(b):
        part = spec2[:, block_columns(b)]
        gram_acc[...] += dot(part, part, NT)

    def gram_of():
        total = gram_acc[...]
        total = total[:K] + total[K:]
        return total[:, :K] + total[:, K:]

    def send_gram(s):
        packed = pack_gram(gram_of())
        gram_send[s] = packed
        gram_recv[s, mj] = packed
        return [
            send(gram_send.at[s], gram_recv.at[s, mj], mz=lax.rem(mj + d, MZ_DEVS))
            for d in range(1, MZ_DEVS)
        ]

    def gram_sum(s, copies):
        for copy in copies:
            copy.wait_recv()
        total = gram_recv[s, 0]
        for j in range(1, MZ_DEVS):
            total = total + gram_recv[s, j]
        return unpack_gram(total)

    spec_load.wait()

    def first_spectra(b, carry):
        columns = block_columns(b)
        upper, lower = split(spec32[:, columns])
        spec2[:K, columns] = upper
        spec2[K:, columns] = lower
        square(b)
        return carry

    lax.fori_loop(0, RING, first_spectra, 0)
    gram_copies = send_gram(0)

    for b in range(RING):
        loads[b].wait()
        columns = pl.ds(b * BLOCK, BLOCK)

        def split_rows(r, carry):
            rows = pl.multiple_of(r * 32, 32)
            upper, lower = split(raw32[pl.ds(rows, 32), columns])
            rows = pl.multiple_of(rows + HALO, HALO)
            high[pl.ds(rows, 32), columns] = upper
            low[pl.ds(rows, 32), columns] = lower
            return carry

        lax.fori_loop(0, ROWS // 32, split_rows, 0)
        part = spec2[:, columns]
        own = pl.ds(HALO, ROWS)
        acc[own, :] += dot(high[own, columns], part, NT) + dot(low[own, columns], part, NT)

    halo_up.wait_recv()
    halo_down.wait_recv()

    def halo_block(b, carry):
        columns = block_columns(b)
        for side, rows in ((0, pl.ds(0, HALO)), (1, pl.ds(HALO + ROWS, HALO))):
            upper, lower = split(halo32[side, :, columns])
            high[rows, columns] = upper
            low[rows, columns] = lower
            halo2[side * HALO : (side + 1) * HALO, :] = upper
            halo2[(side + 2) * HALO : (side + 3) * HALO, :] = lower
        total = dot(halo2[...], spec2[:, columns], NT)
        total = total[: 2 * HALO] + total[2 * HALO :]
        acc[:HALO, :] += total[:HALO]
        acc[HALO + ROWS : PADDED, :] += total[HALO:]
        return carry

    lax.fori_loop(0, RING, halo_block, 0)

    for s in range(SWEEPS):
        for t in range(3):
            part = dot(acc[t * TILE : (t + 2) * TILE, :], warp[t], TN, HIGHEST)
            score_send[s, :, t * TILE : (t + 1) * TILE] = part[:K] + part[K:]
        copies = []
        for d in range(1, MZ_DEVS):
            j = lax.rem(mj + d, MZ_DEVS)
            rows = pl.ds(pl.multiple_of(j * 8, 8), 8)
            copies.append(send(score_send.at[s, rows], score_recv.at[s, d], mz=j))
        gram = gram_sum(s, gram_copies)
        if s > 0:
            eye = iota((K, K), 0) == iota((K, K), 1)
            diagonal = jnp.where(eye, gram, 0.0)
            down = 1.0 / jnp.sqrt(jnp.sum(diagonal, axis=1, keepdims=True) / MZ + rms_epsilon)
            across = 1.0 / jnp.sqrt(jnp.sum(diagonal, axis=0, keepdims=True) / MZ + rms_epsilon)
            gram = gram * down * across
        groups = factor_steps(factor_start(gram), 0, 4)
        own = pl.ds(pl.multiple_of(mj * 8, 8), 8)
        total = score_send[s, own]
        for d in range(1, MZ_DEVS):
            copies[d - 1].wait_recv()
            total = total + score_recv[s, d]
        score_sum[s] = total
        score_all[s, own] = total
        copies = [
            send(score_sum.at[s], score_all.at[s, own], mz=lax.rem(mj + d, MZ_DEVS))
            for d in range(1, MZ_DEVS)
        ]
        inverse = factor_end(factor_steps(groups, 4, 8))
        for copy in copies:
            copy.wait_recv()
        scores = score_all[s]
        if s > 0:
            scores = scores * down
        conc = jnp.maximum(solve(inverse, scores), 0.0)
        if s == SWEEPS - 1:
            conc_out[...] = conc.T

        packed = pack_gram(dot(conc, conc, NT, HIGHEST))
        conc_gram[s] = packed
        gram_copy = send(conc_gram.at[s], conc_gram_core.at[s], rows=partner)

        spread[...] = jnp.zeros_like(spread)
        for t in range(3):
            part = dot(conc[:, t * TILE : (t + 1) * TILE], warp[t], NT, HIGHEST)
            spread[:, t * TILE : (t + 2) * TILE] += part
        upper, lower = split(spread[...])
        spread2[:K] = upper
        spread2[K:] = lower

        core_copies = {}

        def cross_block(i):
            columns = block_columns(at_z(ORDER[i]))
            left = spread2[:, :PADDED]
            part = dot(left, high[:, columns], NN) + dot(left, low[:, columns], NN)
            part = part[:K] + part[K:]
            cross[s, i, 0] = part[:, :HALF]
            cross[s, i, 1] = part[:, HALF:]
            core_copies[i] = send(cross.at[s, i, 1 - core], cross_core.at[s, i], rows=partner)

        def cross_add(i):
            core_copies[i].wait_recv()
            cross[s, i, core] += cross_core[s, i]

        UPPER, LOWER, BOTH = pl.ds(0, K // 2), pl.ds(K // 2, K // 2), pl.ds(0, K)

        def chain_send(step, first, second):
            part = BOTH if step else UPPER
            one = send(cross.at[s, first, core, part], chain_up.at[s, step, part], rows=z_device(1))
            part = BOTH if step else LOWER
            two = send(cross.at[s, second, core, part], chain_down.at[s, step, part], rows=z_device(7))
            return one, two

        def chain_add(step, copies, first, second):
            copies[0].wait_recv()
            part = BOTH if step else UPPER
            cross[s, first, core, part] += chain_up[s, step, part]
            copies[1].wait_recv()
            part = BOTH if step else LOWER
            cross[s, second, core, part] += chain_down[s, step, part]

        cross_block(0)
        cross_block(1)
        cross_block(2)
        cross_add(0)
        chain = chain_send(0, 0, 0)
        gram_copy.wait_recv()
        packed = conc_gram[s] + conc_gram_core[s]
        conc_gram_pair[s] = packed
        gram_copy = send(conc_gram_pair.at[s], conc_gram_y.at[s], rows=y_pair)
        cross_block(3)
        cross_block(4)
        cross_add(1)
        cross_add(2)
        chain_add(0, chain, 1, 2)
        chain = chain_send(1, 1, 2)
        gram_copy.wait_recv()
        packed = conc_gram_pair[s] + conc_gram_y[s]
        conc_gram_all[s, z] = packed
        gram_copies = [
            send(conc_gram_all.at[s, z], conc_gram_all.at[s, z], rows=z_device(d))
            for d in range(1, RING)
        ]
        cross_block(5)
        cross_block(6)
        cross_add(3)
        cross_add(4)
        chain_add(1, chain, 3, 4)
        chain = chain_send(2, 3, 4)
        cross_block(7)
        cross_add(5)
        cross_add(6)
        for copy in gram_copies:
            copy.wait_recv()
        packed = conc_gram_all[s, 0]
        for d in range(1, RING):
            packed = packed + conc_gram_all[s, d]
        groups = factor_steps(factor_start(unpack_gram(packed)), 0, 2)
        chain_add(2, chain, 5, 6)
        chain = chain_send(3, 5, 6)
        cross_add(7)
        groups = factor_steps(groups, 2, 5)
        chain_add(3, chain, 7, 7)
        y_copy = send(cross.at[s, 7, core], cross_y.at[s], rows=y_pair)
        inverse = factor_end(factor_steps(groups, 5, 8))
        y_copy.wait_recv()
        block = cross[s, 7, core] + cross_y[s]
        found[s, core, z] = jnp.maximum(solve(inverse, block), 0.0)

        if s < SWEEPS - 1:
            acc[...] = jnp.zeros_like(acc)
        gram_acc[...] = jnp.zeros_like(gram_acc)

        def to_core(b):
            place = found.at[s, core, b]
            return send(place, place, rows=partner)

        def along(b, distance, part):
            place = found.at[s, core, b, part]
            return send(place, place, rows=z_device(distance))

        def use_block(b):
            columns = block_columns(b)
            if s < SWEEPS - 1:
                for c in range(2):
                    upper, lower = split(found[s, c, b])
                    spec2[:K, pl.ds(pl.multiple_of(b * BLOCK + c * HALF, TILE), HALF)] = upper
                    spec2[K:, pl.ds(pl.multiple_of(b * BLOCK + c * HALF, TILE), HALF)] = lower
                square(b)
                part = spec2[:, columns]
                acc[:PADDED, :] += dot(high[:, columns], part, NT) + dot(low[:, columns], part, NT)
            else:
                for c in range(2):
                    x = found[s, c, b]
                    x = x * x
                    gram_acc[:K, :] += (
                        x[:, :TILE] + x[:, TILE : 2 * TILE] + x[:, 2 * TILE :]
                    )

        up = along(z, 1, BOTH)
        down_way = along(z, 7, BOTH)
        ready = [(z, [to_core(z)])]
        for step in range(1, 5):
            up.wait_recv()
            below, above = at_z(RING - step), at_z(step)
            last = step == 4
            if not last:
                up = along(below, 1, BOTH if step < 3 else UPPER)
            down_way.wait_recv()
            if not last:
                down_way = along(above, 7, BOTH if step < 3 else LOWER)
            arrived = [(below, [to_core(below)])]
            if not last:
                arrived.append((above, [to_core(above)]))
            for b, copies in ready:
                for copy in copies:
                    copy.wait_recv()
                use_block(b)
            ready = arrived
        for b, copies in ready:
            for copy in copies:
                copy.wait_recv()
            use_block(b)
        if s < SWEEPS - 1:
            gram_copies = send_gram(s + 1)

    ones = jnp.ones((8, TILE), F32)
    squares = dot(ones, gram_acc[:K, :], NT, HIGHEST)
    square_recv[MZ_DEVS] = squares
    copies = [
        send(square_recv.at[MZ_DEVS], square_recv.at[mj], mz=lax.rem(mj + d, MZ_DEVS))
        for d in range(1, MZ_DEVS)
    ]
    square_recv[mj] = squares
    for copy in copies:
        copy.wait_recv()
    total = square_recv[0]
    for j in range(1, MZ_DEVS):
        total = total + square_recv[j]
    across = 1.0 / jnp.sqrt(total / MZ + rms_epsilon)
    down = across.T[:, :1]

    def write(b, carry):
        for c in range(2):
            spec_out[:, pl.ds(pl.multiple_of(b * BLOCK + c * HALF, TILE), HALF)] = (
                found[SWEEPS - 1, c, b] * down
            )
        return carry

    lax.fori_loop(0, RING, write, 0)
    for copy in started:
        copy.wait_send()


COPIES = 256


def body(raw_scans, scan_shift, scan_weight, spectra_init):
    any_space = pl.BlockSpec(memory_space=pl.ANY)
    vmem = pl.BlockSpec(memory_space=pltpu.VMEM)
    return pl.pallas_call(
        kernel,
        out_shape=(
            jax.ShapeDtypeStruct((ROWS, K), F32),
            jax.ShapeDtypeStruct((K, COLS), F32),
        ),
        in_specs=[any_space, vmem, vmem, any_space],
        out_specs=(vmem, vmem),
        scratch_shapes=[
            pltpu.VMEM((ROWS, COLS), F32),
            pltpu.VMEM((K, COLS), F32),
            pltpu.VMEM((2, HALO, COLS), F32),
            pltpu.VMEM((PADDED, COLS), BF16),
            pltpu.VMEM((PADDED, COLS), BF16),
            pltpu.VMEM((2 * K, COLS), BF16),
            pltpu.VMEM((4 * HALO, BLOCK), BF16),
            pltpu.VMEM((3, 2 * TILE, TILE), F32),
            pltpu.VMEM((TALL, 2 * K), F32),
            pltpu.VMEM((2 * K, 2 * K), F32),
            pltpu.VMEM((SWEEPS, K // 2, 2 * K), F32),
            pltpu.VMEM((SWEEPS, MZ_DEVS, K // 2, 2 * K), F32),
            pltpu.VMEM((SWEEPS, K, ROWS), F32),
            pltpu.VMEM((SWEEPS, MZ_DEVS, 8, ROWS), F32),
            pltpu.VMEM((SWEEPS, 8, ROWS), F32),
            pltpu.VMEM((SWEEPS, K, ROWS), F32),
            pltpu.VMEM((SWEEPS, K // 2, 2 * K), F32),
            pltpu.VMEM((SWEEPS, K // 2, 2 * K), F32),
            pltpu.VMEM((SWEEPS, K // 2, 2 * K), F32),
            pltpu.VMEM((SWEEPS, K // 2, 2 * K), F32),
            pltpu.VMEM((SWEEPS, RING, K // 2, 2 * K), F32),
            pltpu.VMEM((K, TALL), F32),
            pltpu.VMEM((2 * K, TALL), BF16),
            pltpu.VMEM((SWEEPS, RING, 2, K, HALF), F32),
            pltpu.VMEM((SWEEPS, RING, K, HALF), F32),
            pltpu.VMEM((SWEEPS, 4, K, HALF), F32),
            pltpu.VMEM((SWEEPS, 4, K, HALF), F32),
            pltpu.VMEM((SWEEPS, K, HALF), F32),
            pltpu.VMEM((SWEEPS, 2, RING, K, HALF), F32),
            pltpu.VMEM((MZ_DEVS + 1, 8, K), F32),
            pltpu.SemaphoreType.DMA((RING + 1,)),
            pltpu.SemaphoreType.DMA((COPIES,)),
            pltpu.SemaphoreType.DMA((COPIES,)),
        ],
        compiler_params=pltpu.CompilerParams(
            collective_id=0, has_side_effects=True, vmem_limit_bytes=56 * 1024 * 1024
        ),
        name="mcr_als",
    )(raw_scans, scan_shift.reshape(1, ROWS), scan_weight.reshape(1, ROWS), spectra_init)


def solution(mesh):
    return jax.shard_map(
        body,
        mesh=mesh,
        in_specs=(P("rows", "mz"), P("rows"), P("rows"), P(None, "mz")),
        out_specs=(P("rows", None), P(None, "mz")),
        check_vma=False,
    )
```

```python
import functools

import jax
import jax.numpy as jnp
from jax import lax
from jax.experimental import pallas as pl
from jax.experimental.pallas import tpu as pltpu
from jax.sharding import PartitionSpec as P

MESH = pl.DeviceIdType.MESH
F32 = jnp.float32
BF16 = jnp.bfloat16

MZ = 49152
K = 64
HALO = 16
SWEEPS = 2
ROW_DEVS = 32
MZ_DEVS = 8
RING = 8
ROWS = 384
PADDED = ROWS + 2 * HALO
TALL = 512
COLS = 6144
BLOCK = COLS // RING
HALF = BLOCK // 2
TILE = 128
HALO_PARTS = 2
LOADS = 4

fraction_unit = 256.0
rms_epsilon = 1e-06
ridge_share = 0.01

ORDER = (4, 3, 5, 2, 6, 1, 7, 0)
WAYS = ((1, 2), (7, 6))
HALVES = (pl.ds(0, K // 4), pl.ds(K // 4, K // 4))


def split(x):
    high = x.astype(BF16)
    return high, (x - high.astype(F32)).astype(BF16)


def dot(left, right, dims, precision=None):
    return lax.dot_general(
        left, right, (dims, ((), ())), precision=precision, preferred_element_type=F32
    )


NN = ((1,), (0,))
NT = ((1,), (1,))
TN = ((0,), (0,))
HIGHEST = lax.Precision.HIGHEST


def iota(shape, dim):
    return lax.broadcasted_iota(jnp.int32, shape, dim)


def pack_gram(gram):
    return jnp.concatenate([gram[: K // 2], gram[K // 2 :]], axis=1)


def unpack_gram(packed):
    return jnp.concatenate([packed[:, :K], packed[:, K:]], axis=0)


def factor_start(gram):
    eye = iota((K, K), 0) == iota((K, K), 1)
    diagonal = jnp.where(eye, gram, 0.0)
    trace = jnp.sum(jnp.sum(diagonal, axis=1, keepdims=True), axis=0, keepdims=True)
    ridge = ridge_share * trace / K
    unit = jnp.where(eye, 1.0, 0.0).astype(F32)
    joined = jnp.concatenate([gram + unit * ridge, unit], axis=1)
    return tuple(joined[8 * j : 8 * j + 8] for j in range(8))


def factor_steps(groups, first, last):
    sub = iota((8, 2 * K), 0)
    shape = (8, 2 * K)

    def step(g, groups):
        head = groups[0]
        columns = [jnp.broadcast_to(head[:, p : p + 1], shape) for p in range(8)]
        square = {}
        for p in range(8):
            for q in range(p, 8):
                square[q, p] = jnp.broadcast_to(columns[p][q : q + 1], shape)
        rows = [jnp.broadcast_to(head[p : p + 1], shape) for p in range(8)]
        inverse = []
        ratio = {}
        for p in range(8):
            inverse.append(1.0 / square[p, p])
            for q in range(p + 1, 8):
                ratio[q, p] = square[q, p] * inverse[p]
                for r in range(p + 1, q + 1):
                    square[q, r] = square[q, r] - ratio[q, p] * square[r, p]
                rows[q] = rows[q] - ratio[q, p] * rows[p]
        scaled = [rows[p] * inverse[p] for p in range(8)]
        done = rows[0]
        for p in range(8):
            root = lax.rsqrt(square[p, p])
            root = root * (1.5 - 0.5 * square[p, p] * root * root)
            done = jnp.where(sub == p, rows[p] * root, done)
        rest = []
        for j in range(1, 8):
            left = [groups[j][:, p : p + 1] for p in range(8)]
            left = [jnp.broadcast_to(x, shape) for x in left]
            for p in range(7):
                for q in range(p + 1, 8):
                    left[q] = left[q] - ratio[q, p] * left[p]
            terms = [left[p] * scaled[p] for p in range(8)]
            while len(terms) > 1:
                terms = [terms[i] + terms[i + 1] for i in range(0, len(terms), 2)]
            rest.append(groups[j] - jnp.where(j < 8 - g, terms[0], 0.0))
        return tuple(pltpu.roll(x, 2 * K - 8, 1) for x in rest + [done])

    return lax.fori_loop(first, last, step, groups)


def factor_end(groups):
    return jnp.concatenate(groups, axis=0)[:, :K]


def solve(inverse_factor, target):
    return dot(inverse_factor, dot(inverse_factor, target, NN, HIGHEST), TN, HIGHEST)


def kernel(
    raw, shift, weight, spec, conc_out, spec_out, scale_out,
    raw32, spec32, halo32, high, low, spec2, halo2, warp, acc,
    gram_send, gram_recv, score_send, score_recv, score_sum, score_all,
    conc_gram, conc_gram_core, conc_gram_pair, conc_gram_y, conc_gram_all, conc_gram_sum, conc_gram_total,
    spread, spread2, cross, cross_core, cross_y, far, farther, near, next_to, summed, owned,
    found, square_send, square_mz, square_z, square_y, load_sem, store_sem, send_sem, recv_sem,
):
    ri = lax.axis_index("rows")
    mj = lax.axis_index("mz")
    core = lax.rem(ri, 2)
    z = lax.rem(lax.div(ri, 2), RING)
    plane = ri - 2 * z

    def at_z(distance):
        return lax.rem(z + distance, RING)

    def z_device(distance):
        return plane + 2 * at_z(distance)

    def other_plane(device):
        return lax.rem(device + 16, ROW_DEVS)

    partner = ri + 1 - 2 * core
    y = lax.div(ri, 16)
    y_pair = lax.rem(ri + 16, ROW_DEVS)
    row_next = lax.rem(ri + 1, ROW_DEVS)
    row_back = lax.rem(ri + ROW_DEVS - 1, ROW_DEVS)
    started = []
    settled = []
    stores = []

    def send(source, target, rows=None, mz=None):
        number = len(started)
        copy = pltpu.make_async_remote_copy(
            src_ref=source,
            dst_ref=target,
            send_sem=send_sem.at[number],
            recv_sem=recv_sem.at[number],
            device_id=(ri if rows is None else rows, mj if mz is None else mz),
            device_id_type=MESH,
        )
        copy.start()
        started.append(copy)
        return copy

    def settle(keep):
        while len(settled) < len(started) - keep:
            started[len(settled)].wait_send()
            settled.append(True)

    def to_mz(source, target):
        return [
            send(source, target, mz=lax.rem(mj + d, MZ_DEVS)) for d in range(1, MZ_DEVS)
        ]

    def to_z(source, target):
        return [send(source, target, rows=z_device(d)) for d in range(1, RING)]

    def sum_slots(slots, count, copies):
        for copy in copies:
            copy.wait_recv()
        total = slots[0]
        for j in range(1, count):
            total = total + slots[j]
        return total

    def block_columns(b):
        return pl.ds(pl.multiple_of(b * BLOCK, TILE), BLOCK)

    spec_load = pltpu.make_async_copy(spec, spec32, load_sem.at[LOADS])
    spec_load.start()
    loads = []
    for b in range(LOADS):
        columns = pl.ds(b * (COLS // LOADS), COLS // LOADS)
        loads.append(pltpu.make_async_copy(raw.at[:, columns], raw32.at[:, columns], load_sem.at[b]))
        loads[-1].start()

    barrier = pltpu.get_barrier_semaphore()
    peers = [(ri, lax.rem(mj + d, MZ_DEVS)) for d in range(1, MZ_DEVS)]
    peers += [(z_device(d), mj) for d in range(1, RING)]
    peers += [(other_plane(z_device(d)), mj) for d in (1, 2, 6, 7)]
    peers += [(y_pair, mj), (row_next, mj), (row_back, mj)]
    for peer in peers:
        pl.semaphore_signal(barrier, inc=1, device_id=peer, device_id_type=MESH)

    pl.semaphore_wait(barrier, len(peers))
    halos = []
    for part in range(HALO_PARTS):
        columns = pl.ds(part * (COLS // HALO_PARTS), COLS // HALO_PARTS)
        halos.append((
            send(raw.at[pl.ds(ROWS - HALO, HALO), columns], halo32.at[0, :, columns], rows=row_next),
            send(raw.at[pl.ds(0, HALO), columns], halo32.at[1, :, columns], rows=row_back),
        ))

    for t in range(3):
        tile = pl.ds(t * TILE, TILE)
        target = iota((2 * TILE, TILE), 1) + shift[tile].reshape(1, TILE) + HALO
        fraction = weight[tile].reshape(1, TILE).astype(F32) / fraction_unit
        row = iota((2 * TILE, TILE), 0)
        warp[t] = jnp.where(row == target, 1.0 - fraction, 0.0) + jnp.where(
            row == target + 1, fraction, 0.0
        )
    acc[...] = jnp.zeros_like(acc)

    def send_gram(s):
        total = dot(spec2[...], spec2[...], NT)
        total = total[:K] + total[K:]
        packed = pack_gram(total[:, :K] + total[:, K:])
        gram_send[s] = packed
        gram_recv[s, mj] = packed
        return to_mz(gram_send.at[s], gram_recv.at[s, mj])

    spec_load.wait()

    def first_spectra(b, carry):
        columns = block_columns(b)
        upper, lower = split(spec32[:, columns])
        spec2[:K, columns] = upper
        spec2[K:, columns] = lower
        return carry

    lax.fori_loop(0, RING, first_spectra, 0)

    gram_copies = send_gram(0)

    for b in range(LOADS):
        loads[b].wait()
        columns = pl.ds(b * (COLS // LOADS), COLS // LOADS)

        def split_rows(r, carry):
            rows = pl.multiple_of(r * HALO, HALO)
            upper, lower = split(raw32[pl.ds(rows, HALO), columns])
            rows = pl.multiple_of(rows + HALO, HALO)
            high[pl.ds(rows, HALO), columns] = upper
            low[pl.ds(rows, HALO), columns] = lower
            return carry

        lax.fori_loop(0, ROWS // 16, split_rows, 0)
        part = spec2[:, columns]
        own = pl.ds(HALO, ROWS)
        acc[own, :] += dot(high[own, columns], part, NT) + dot(low[own, columns], part, NT)

    for part in range(HALO_PARTS):
        for copy in halos[part]:
            copy.wait_recv()
        columns = pl.ds(part * (COLS // HALO_PARTS), COLS // HALO_PARTS)
        for side, rows in ((0, pl.ds(0, HALO)), (1, pl.ds(HALO + ROWS, HALO))):
            upper, lower = split(halo32[side, :, columns])
            high[rows, columns] = upper
            low[rows, columns] = lower
            halo2[side * HALO : (side + 1) * HALO, :] = upper
            halo2[(side + 2) * HALO : (side + 3) * HALO, :] = lower
        total = dot(halo2[...], spec2[:, columns], NT)
        total = total[: 2 * HALO] + total[2 * HALO :]
        acc[:HALO, :] += total[:HALO]
        acc[HALO + ROWS : PADDED, :] += total[HALO:]

    for s in range(SWEEPS):
        last_sweep = s == SWEEPS - 1
        for t in range(3):
            part = dot(acc[t * TILE : (t + 2) * TILE, :], warp[t], TN, HIGHEST)
            score_send[s, :, t * TILE : (t + 1) * TILE] = part[:K] + part[K:]
        copies = []
        for d in range(1, MZ_DEVS):
            j = lax.rem(mj + d, MZ_DEVS)
            rows = pl.ds(pl.multiple_of(j * 8, 8), 8)
            copies.append(send(score_send.at[s, rows], score_recv.at[s, d], mz=j))
        if s > 0:
            gram_copies = send_gram(s)
        if s == 0:
            gram = unpack_gram(sum_slots(gram_recv.at[s], MZ_DEVS, gram_copies))
            inverse = factor_end(factor_steps(factor_start(gram), 0, 8))
        own = pl.ds(pl.multiple_of(mj * 8, 8), 8)
        total = score_send[s, own]
        for d in range(1, MZ_DEVS):
            copies[d - 1].wait_recv()
            total = total + score_recv[s, d]
        score_sum[s] = total
        score_all[s, own] = total
        copies = to_mz(score_sum.at[s], score_all.at[s, own])
        if s > 0:
            gram = unpack_gram(sum_slots(gram_recv.at[s], MZ_DEVS, gram_copies))
            eye = iota((K, K), 0) == iota((K, K), 1)
            diagonal = jnp.where(eye, gram, 0.0)
            down = 1.0 / jnp.sqrt(jnp.sum(diagonal, axis=1, keepdims=True) / MZ + rms_epsilon)
            across = 1.0 / jnp.sqrt(jnp.sum(diagonal, axis=0, keepdims=True) / MZ + rms_epsilon)
            gram = gram * down * across
            inverse = factor_end(factor_steps(factor_start(gram), 0, 8))
        settle(14)
        for copy in copies:
            copy.wait_recv()
        scores = score_all[s]
        if s > 0:
            scores = scores * down
        conc = jnp.maximum(solve(inverse, scores), 0.0)
        if last_sweep:
            conc_out[...] = conc

        spread[...] = jnp.zeros_like(spread)
        for t in range(3):
            part = dot(conc[:, t * TILE : (t + 1) * TILE], warp[t], NT, HIGHEST)
            spread[:, t * TILE : (t + 2) * TILE] += part
        upper, lower = split(spread[...])
        spread2[:K] = upper
        spread2[K:] = lower

        packed = pack_gram(dot(conc, conc, NT, HIGHEST))
        conc_gram[s] = packed
        gram_copy = send(conc_gram.at[s], conc_gram_core.at[s], rows=partner)

        core_copies = {}
        y_copies = {}

        def cross_blocks(*several):
            for i in several:
                columns = block_columns(at_z(ORDER[i]))
                left = spread2[:, :PADDED]
                part = dot(left, high[:, columns], NN) + dot(left, low[:, columns], NN)
                part = part[:K] + part[K:]
                for c in range(2):
                    for h in range(2):
                        cross[s, i, c, h] = part[c * 32 : c * 32 + 32, h * HALF : h * HALF + HALF]
            for i in several:
                core_copies[i] = send(
                    cross.at[s, i, 1 - core], cross_core.at[s, i], rows=partner
                )

        def cross_add(i):
            core_copies[i].wait_recv()
            cross[s, i, core] += cross_core[s, i]

        def to_y(i):
            y_copies[i] = send(cross.at[s, i, core, 1 - y], cross_y.at[s, i], rows=y_pair)

        def y_sum(i):
            y_copies[i].wait_recv()
            return cross[s, i, core, y] + cross_y[s, i]

        cross_blocks(0)
        cross_blocks(1, 2)
        cross_add(0)
        farther_copies = []
        for way in range(2):
            device = z_device(WAYS[way][1])
            farther_copies += [
                send(cross.at[s, 0, core, y, HALVES[way]], farther.at[s, way, 0], rows=device),
                send(
                    cross.at[s, 0, core, 1 - y, HALVES[way]],
                    farther.at[s, way, 1],
                    rows=other_plane(device),
                ),
            ]
        gram_copy.wait_recv()
        packed = conc_gram[s] + conc_gram_core[s]
        conc_gram_pair[s] = packed
        gram_copy = send(conc_gram_pair.at[s], conc_gram_y.at[s], rows=y_pair)
        far_copies = []
        for way in range(2):
            cross_add(1 + way)
            device = z_device(WAYS[way][0])
            far_copies += [
                send(cross.at[s, 1 + way, core, y], far.at[s, way, 0], rows=device),
                send(
                    cross.at[s, 1 + way, core, 1 - y], far.at[s, way, 1], rows=other_plane(device)
                ),
            ]
        cross_blocks(3, 4)
        cross_blocks(5, 6)
        for i in (3, 4):
            cross_add(i)
            to_y(i)
        gram_copy.wait_recv()
        packed = conc_gram_pair[s] + conc_gram_y[s]
        conc_gram_total[...] = packed
        part = conc_gram_total[pl.ds(pl.multiple_of(16 * core, 16), 16)]
        conc_gram_all[s, z] = part
        gram_copies = to_z(conc_gram_all.at[s, z], conc_gram_all.at[s, z])
        cross_blocks(7)
        for i in (5, 6, 7):
            cross_add(i)
            to_y(i)
        near_copies = []
        for way in range(2):
            total = y_sum(3 + way)
            for plane_copy in range(2):
                far_copies[2 * way + plane_copy].wait_recv()
                total = total + far[s, way, plane_copy]
            summed[s, 3 + way] = total
            for plane_copy in range(2):
                farther_copies[2 * way + plane_copy].wait_recv()
                summed[s, 3 + way, HALVES[way]] += farther[s, way, plane_copy]
            near_copies.append(
                send(summed.at[s, 3 + way], near.at[s, way], rows=z_device(WAYS[way][1]))
            )
        conc_gram_sum[s, core] = sum_slots(conc_gram_all.at[s], RING, gram_copies)
        gram_copy = send(conc_gram_sum.at[s, core], conc_gram_sum.at[s, core], rows=partner)
        next_copies = []
        for way in range(2):
            summed[s, 5 + way] = y_sum(5 + way)
            next_copies.append(
                send(summed.at[s, 5 + way], next_to.at[s, way], rows=z_device(WAYS[way][0]))
            )
        gram_copy.wait_recv()
        groups = factor_steps(
            factor_start(unpack_gram(conc_gram_sum[s].reshape(K // 2, 2 * K))), 0, 6
        )
        total = y_sum(7)
        for way in range(2):
            near_copies[way].wait_recv()
            total = total + near[s, way]
        for way in range(2):
            next_copies[way].wait_recv()
            total = total + next_to[s, way]
        owned[s, core] = total
        owned_copy = send(owned.at[s, core], owned.at[s, core], rows=partner)
        inverse = factor_end(factor_steps(groups, 6, 8))
        settle(16)
        owned_copy.wait_recv()
        block = jnp.maximum(solve(inverse, owned[s].reshape(K, HALF)), 0.0)
        found[s, :, z, y] = block.reshape(2, K // 2, HALF)

        def pass_on(b, device, rows=None, planes=None):
            place = found.at[s, core, b, y if planes is None else planes]
            if rows is not None:
                place = place.at[rows]
            return send(place, place, rows=device)

        def to_core(b):
            place = found.at[s, core, b]
            return send(place, place, rows=partner)

        def use_blocks(*several):
            for b in several:
                for c in range(2):
                    for h in range(2):
                        first = pl.multiple_of(b * BLOCK + h * HALF, TILE)
                        columns = pl.ds(first, HALF)
                        rows = pl.ds(c * 32, 32)
                        if last_sweep:
                            store = pltpu.make_async_copy(
                                found.at[s, c, b, h],
                                spec_out.at[rows, columns],
                                store_sem.at[len(stores)],
                            )
                            store.start()
                            stores.append(store)
                        else:
                            upper, lower = split(found[s, c, b, h])
                            spec2[rows, columns] = upper
                            spec2[pl.ds(K + c * 32, 32), columns] = lower
            if not last_sweep:
                total = acc[:PADDED, :]
                for b in several:
                    columns = block_columns(b)
                    part = spec2[:, columns]
                    total = total + dot(high[:, columns], part, NT)
                    total = total + dot(low[:, columns], part, NT)
                acc[:PADDED, :] = total

        one_away = [pass_on(z, z_device(WAYS[way][0])) for way in range(2)]
        two_away = [pass_on(z, z_device(WAYS[way][1])) for way in range(2)]
        over_y = [pass_on(z, y_pair)]
        if last_sweep:
            x = block * block
            x = x[:, :TILE] + x[:, TILE : 2 * TILE] + x[:, 2 * TILE :]
            squares = dot(jnp.ones((8, TILE), F32), x, NT, HIGHEST)
            square_send[0] = squares
            square_mz[mj] = squares
            square_copies = to_mz(square_send.at[0], square_mz.at[mj])
        else:
            acc[...] = jnp.zeros_like(acc)
        ones = [at_z(RING - 1), at_z(1)]
        twos = [at_z(RING - 2), at_z(2)]
        threes = [at_z(RING - 3), at_z(3)]
        four = at_z(4)
        for way in range(2):
            one_away[way].wait_recv()
            over_y.append(pass_on(ones[way], y_pair))
        three_away, four_away = [], []
        for way in range(2):
            two_away[way].wait_recv()
            device = z_device(WAYS[way][0])
            three_away.append(pass_on(twos[way], device))
            three_away.append(pass_on(twos[way], other_plane(device)))
            device = z_device(WAYS[way][1])
            four_away.append(pass_on(twos[way], device, HALVES[way]))
            four_away.append(pass_on(twos[way], other_plane(device), HALVES[way]))
            over_y.append(pass_on(twos[way], y_pair))
        over_y[0].wait_recv()
        over_core = [pass_on(z, partner, planes=1 - y)]
        if last_sweep:
            squares = sum_slots(square_mz, MZ_DEVS, square_copies)
            square_z[z] = squares
            square_copies = to_z(square_z.at[z], square_z.at[z])
        for way in range(2):
            over_y[1 + way].wait_recv()
            over_core.append(to_core(ones[way]))
        over_core[0].wait_recv()
        use_blocks(z)
        for way in range(2):
            over_y[3 + way].wait_recv()
            over_core.append(to_core(twos[way]))
        for way in range(2):
            over_core[1 + way].wait_recv()
        use_blocks(*ones)
        for way in range(2):
            three_away[2 * way].wait_recv()
            three_away[2 * way + 1].wait_recv()
            over_core.append(to_core(threes[way]))
        if last_sweep:
            squares = sum_slots(square_z, RING, square_copies)
            square_send[1] = squares
            square_copy = send(square_send.at[1], square_y, rows=y_pair)
        for copy in four_away:
            copy.wait_recv()
        over_core.append(to_core(four))
        for way in range(2):
            over_core[3 + way].wait_recv()
        use_blocks(*twos)
        for way in range(2):
            over_core[5 + way].wait_recv()
        over_core[7].wait_recv()
        use_blocks(*threes, four)
        if last_sweep:
            settle(12)

    square_copy.wait_recv()
    across = 1.0 / jnp.sqrt((squares + square_y[...]) / MZ + rms_epsilon)
    scale_out[...] = across[0]
    for store in stores:
        store.wait()
    settle(0)


COPIES = 200


def body(raw_scans, scan_shift, scan_weight, spectra_init):
    any_space = pl.BlockSpec(memory_space=pl.ANY)
    vmem = pl.BlockSpec(memory_space=pltpu.VMEM)
    conc, spectra, scale = pl.pallas_call(
        kernel,
        out_shape=(
            jax.ShapeDtypeStruct((K, ROWS), F32),
            jax.ShapeDtypeStruct((K, COLS), F32),
            jax.ShapeDtypeStruct((K,), F32),
        ),
        in_specs=[any_space, vmem, vmem, any_space],
        out_specs=(vmem, any_space, vmem),
        scratch_shapes=[
            pltpu.VMEM((ROWS, COLS), F32),
            pltpu.VMEM((K, COLS), F32),
            pltpu.VMEM((2, HALO, COLS), F32),
            pltpu.VMEM((PADDED, COLS), BF16),
            pltpu.VMEM((PADDED, COLS), BF16),
            pltpu.VMEM((2 * K, COLS), BF16),
            pltpu.VMEM((4 * HALO, COLS // HALO_PARTS), BF16),
            pltpu.VMEM((3, 2 * TILE, TILE), F32),
            pltpu.VMEM((TALL, 2 * K), F32),
            pltpu.VMEM((SWEEPS, K // 2, 2 * K), F32),
            pltpu.VMEM((SWEEPS, MZ_DEVS, K // 2, 2 * K), F32),
            pltpu.VMEM((SWEEPS, K, ROWS), F32),
            pltpu.VMEM((SWEEPS, MZ_DEVS, 8, ROWS), F32),
            pltpu.VMEM((SWEEPS, 8, ROWS), F32),
            pltpu.VMEM((SWEEPS, K, ROWS), F32),
            pltpu.VMEM((SWEEPS, K // 2, 2 * K), F32),
            pltpu.VMEM((SWEEPS, K // 2, 2 * K), F32),
            pltpu.VMEM((SWEEPS, K // 2, 2 * K), F32),
            pltpu.VMEM((SWEEPS, K // 2, 2 * K), F32),
            pltpu.VMEM((SWEEPS, RING, K // 4, 2 * K), F32),
            pltpu.VMEM((SWEEPS, 2, K // 4, 2 * K), F32),
            pltpu.VMEM((K // 2, 2 * K), F32),
            pltpu.VMEM((K, TALL), F32),
            pltpu.VMEM((2 * K, TALL), BF16),
            pltpu.VMEM((SWEEPS, RING, 2, 2, K // 2, HALF), F32),
            pltpu.VMEM((SWEEPS, RING, 2, K // 2, HALF), F32),
            pltpu.VMEM((SWEEPS, RING, K // 2, HALF), F32),
            pltpu.VMEM((SWEEPS, 2, 2, K // 2, HALF), F32),
            pltpu.VMEM((SWEEPS, 2, 2, K // 4, HALF), F32),
            pltpu.VMEM((SWEEPS, 2, K // 2, HALF), F32),
            pltpu.VMEM((SWEEPS, 2, K // 2, HALF), F32),
            pltpu.VMEM((SWEEPS, RING, K // 2, HALF), F32),
            pltpu.VMEM((SWEEPS, 2, K // 2, HALF), F32),
            pltpu.VMEM((SWEEPS, 2, RING, 2, K // 2, HALF), F32),
            pltpu.VMEM((2, 8, K), F32),
            pltpu.VMEM((MZ_DEVS, 8, K), F32),
            pltpu.VMEM((RING, 8, K), F32),
            pltpu.VMEM((8, K), F32),
            pltpu.SemaphoreType.DMA((LOADS + 1,)),
            pltpu.SemaphoreType.DMA((4 * RING,)),
            pltpu.SemaphoreType.DMA((COPIES,)),
            pltpu.SemaphoreType.DMA((COPIES,)),
        ],
        compiler_params=pltpu.CompilerParams(
            collective_id=0, has_side_effects=True, vmem_limit_bytes=56 * 1024 * 1024
        ),
        name="mcr_als",
    )(raw_scans, scan_shift, scan_weight, spectra_init)
    return conc.T, spectra * scale[:, None]


def solution(mesh):
    return jax.shard_map(
        body,
        mesh=mesh,
        in_specs=(P("rows", "mz"), P("rows"), P("rows"), P(None, "mz")),
        out_specs=(P("rows", None), P(None, "mz")),
        check_vma=False,
    )
```

```python
import functools

import jax
import jax.numpy as jnp
from jax import lax
from jax.experimental import pallas as pl
from jax.experimental.pallas import tpu as pltpu
from jax.sharding import PartitionSpec as P

MESH = pl.DeviceIdType.MESH
F32 = jnp.float32
BF16 = jnp.bfloat16

MZ = 49152
K = 64
HALO = 16
SWEEPS = 2
ROW_DEVS = 32
MZ_DEVS = 8
RING = 8
ROWS = 384
PADDED = ROWS + 2 * HALO
TALL = 512
COLS = 6144
BLOCK = COLS // RING
HALF = BLOCK // 2
TILE = 128
HALO_PARTS = 2
LOADS = 4

fraction_unit = 256.0
rms_epsilon = 1e-06
ridge_share = 0.01

ORDER = (4, 3, 5, 2, 6, 1, 7, 0)
WAYS = ((1, 2), (7, 6))
HALVES = (pl.ds(0, K // 4), pl.ds(K // 4, K // 4))


def split(x):
    high = x.astype(BF16)
    return high, (x - high.astype(F32)).astype(BF16)


def dot(left, right, dims, precision=None):
    return lax.dot_general(
        left, right, (dims, ((), ())), precision=precision, preferred_element_type=F32
    )


NN = ((1,), (0,))
NT = ((1,), (1,))
TN = ((0,), (0,))
HIGHEST = lax.Precision.HIGHEST


def iota(shape, dim):
    return lax.broadcasted_iota(jnp.int32, shape, dim)


def pack_gram(gram):
    return jnp.concatenate([gram[: K // 2], gram[K // 2 :]], axis=1)


def unpack_gram(packed):
    return jnp.concatenate([packed[:, :K], packed[:, K:]], axis=0)


def factor_start(gram):
    eye = iota((K, K), 0) == iota((K, K), 1)
    diagonal = jnp.where(eye, gram, 0.0)
    trace = jnp.sum(jnp.sum(diagonal, axis=1, keepdims=True), axis=0, keepdims=True)
    ridge = ridge_share * trace / K
    unit = jnp.where(eye, 1.0, 0.0).astype(F32)
    joined = jnp.concatenate([gram + unit * ridge, unit], axis=1)
    return tuple(joined[8 * j : 8 * j + 8] for j in range(8))


def factor_steps(groups, first, last):
    sub = iota((8, 2 * K), 0)
    shape = (8, 2 * K)

    def step(g, groups):
        head = groups[0]
        columns = [jnp.broadcast_to(head[:, p : p + 1], shape) for p in range(8)]
        square = {}
        for p in range(8):
            for q in range(p, 8):
                square[q, p] = jnp.broadcast_to(columns[p][q : q + 1], shape)
        rows = [jnp.broadcast_to(head[p : p + 1], shape) for p in range(8)]
        inverse = []
        ratio = {}
        for p in range(8):
            inverse.append(1.0 / square[p, p])
            for q in range(p + 1, 8):
                ratio[q, p] = square[q, p] * inverse[p]
                for r in range(p + 1, q + 1):
                    square[q, r] = square[q, r] - ratio[q, p] * square[r, p]
                rows[q] = rows[q] - ratio[q, p] * rows[p]
        scaled = [rows[p] * inverse[p] for p in range(8)]
        done = rows[0]
        for p in range(8):
            root = lax.rsqrt(square[p, p])
            root = root * (1.5 - 0.5 * square[p, p] * root * root)
            done = jnp.where(sub == p, rows[p] * root, done)
        rest = []
        for j in range(1, 8):
            left = [groups[j][:, p : p + 1] for p in range(8)]
            left = [jnp.broadcast_to(x, shape) for x in left]
            for p in range(7):
                for q in range(p + 1, 8):
                    left[q] = left[q] - ratio[q, p] * left[p]
            terms = [left[p] * scaled[p] for p in range(8)]
            while len(terms) > 1:
                terms = [terms[i] + terms[i + 1] for i in range(0, len(terms), 2)]
            rest.append(groups[j] - jnp.where(j < 8 - g, terms[0], 0.0))
        return tuple(pltpu.roll(x, 2 * K - 8, 1) for x in rest + [done])

    return lax.fori_loop(first, last, step, groups)


def factor_end(groups):
    return jnp.concatenate(groups, axis=0)[:, :K]


def solve(inverse_factor, target):
    return dot(inverse_factor, dot(inverse_factor, target, NN, HIGHEST), TN, HIGHEST)


def kernel(
    raw, shift, weight, spec, conc_out, spec_out, scale_out,
    raw32, spec32, halo32, high, low, spec2, halo2, warp, acc,
    gram_send, gram_recv, score_send, score_recv, score_sum, score_all,
    conc_gram, conc_gram_core, conc_gram_pair, conc_gram_y, conc_gram_all, conc_gram_sum, conc_gram_total,
    spread, spread2, cross, cross_core, cross_y, far, farther, near, next_to, summed, owned,
    found, square_send, square_mz, square_z, square_y, load_sem, store_sem, send_sem, recv_sem,
):
    ri = lax.axis_index("rows")
    mj = lax.axis_index("mz")
    core = lax.rem(ri, 2)
    z = lax.rem(lax.div(ri, 2), RING)
    plane = ri - 2 * z

    def at_z(distance):
        return lax.rem(z + distance, RING)

    def z_device(distance):
        return plane + 2 * at_z(distance)

    def other_plane(device):
        return lax.rem(device + 16, ROW_DEVS)

    partner = ri + 1 - 2 * core
    y = lax.div(ri, 16)
    y_pair = lax.rem(ri + 16, ROW_DEVS)
    row_next = lax.rem(ri + 1, ROW_DEVS)
    row_back = lax.rem(ri + ROW_DEVS - 1, ROW_DEVS)
    started = []
    settled = []
    stores = []

    def send(source, target, rows=None, mz=None):
        number = len(started)
        copy = pltpu.make_async_remote_copy(
            src_ref=source,
            dst_ref=target,
            send_sem=send_sem.at[number],
            recv_sem=recv_sem.at[number],
            device_id=(ri if rows is None else rows, mj if mz is None else mz),
            device_id_type=MESH,
        )
        copy.start()
        started.append(copy)
        return copy

    def settle(keep):
        while len(settled) < len(started) - keep:
            started[len(settled)].wait_send()
            settled.append(True)

    def to_mz(source, target):
        return [
            send(source, target, mz=lax.rem(mj + d, MZ_DEVS)) for d in range(1, MZ_DEVS)
        ]

    def to_z(source, target):
        return [send(source, target, rows=z_device(d)) for d in range(1, RING)]

    def sum_slots(slots, count, copies):
        for copy in copies:
            copy.wait_recv()
        total = slots[0]
        for j in range(1, count):
            total = total + slots[j]
        return total

    def block_columns(b):
        return pl.ds(pl.multiple_of(b * BLOCK, TILE), BLOCK)

    spec_load = pltpu.make_async_copy(spec, spec32, load_sem.at[LOADS])
    spec_load.start()
    loads = []
    for b in range(LOADS):
        columns = pl.ds(b * (COLS // LOADS), COLS // LOADS)
        loads.append(pltpu.make_async_copy(raw.at[:, columns], raw32.at[:, columns], load_sem.at[b]))
        loads[-1].start()

    barrier = pltpu.get_barrier_semaphore()
    peers = [(ri, lax.rem(mj + d, MZ_DEVS)) for d in range(1, MZ_DEVS)]
    peers += [(z_device(d), mj) for d in range(1, RING)]
    peers += [(other_plane(z_device(d)), mj) for d in (1, 2, 6, 7)]
    peers += [(y_pair, mj), (row_next, mj), (row_back, mj)]
    for peer in peers:
        pl.semaphore_signal(barrier, inc=1, device_id=peer, device_id_type=MESH)

    pl.semaphore_wait(barrier, len(peers))
    halos = []
    for part in range(HALO_PARTS):
        columns = pl.ds(part * (COLS // HALO_PARTS), COLS // HALO_PARTS)
        halos.append((
            send(raw.at[pl.ds(ROWS - HALO, HALO), columns], halo32.at[0, :, columns], rows=row_next),
            send(raw.at[pl.ds(0, HALO), columns], halo32.at[1, :, columns], rows=row_back),
        ))

    for t in range(3):
        tile = pl.ds(t * TILE, TILE)
        target = iota((2 * TILE, TILE), 1) + shift[tile].reshape(1, TILE) + HALO
        fraction = weight[tile].reshape(1, TILE).astype(F32) / fraction_unit
        row = iota((2 * TILE, TILE), 0)
        warp[t] = jnp.where(row == target, 1.0 - fraction, 0.0) + jnp.where(
            row == target + 1, fraction, 0.0
        )
    acc[...] = jnp.zeros_like(acc)

    def send_gram(s):
        total = dot(spec2[...], spec2[...], NT)
        total = total[:K] + total[K:]
        packed = pack_gram(total[:, :K] + total[:, K:])
        gram_send[s] = packed
        gram_recv[s, mj] = packed
        return to_mz(gram_send.at[s], gram_recv.at[s, mj])

    spec_load.wait()

    def first_spectra(b, carry):
        columns = block_columns(b)
        upper, lower = split(spec32[:, columns])
        spec2[:K, columns] = upper
        spec2[K:, columns] = lower
        return carry

    lax.fori_loop(0, RING, first_spectra, 0)

    gram_copies = send_gram(0)

    for b in range(LOADS):
        loads[b].wait()
        columns = pl.ds(b * (COLS // LOADS), COLS // LOADS)

        def split_rows(r, carry):
            rows = pl.multiple_of(r * HALO, HALO)
            upper, lower = split(raw32[pl.ds(rows, HALO), columns])
            rows = pl.multiple_of(rows + HALO, HALO)
            high[pl.ds(rows, HALO), columns] = upper
            low[pl.ds(rows, HALO), columns] = lower
            return carry

        lax.fori_loop(0, ROWS // 16, split_rows, 0)
        part = spec2[:, columns]
        own = pl.ds(HALO, ROWS)
        acc[own, :] += dot(high[own, columns], part, NT) + dot(low[own, columns], part, NT)

    for part in range(HALO_PARTS):
        for copy in halos[part]:
            copy.wait_recv()
        columns = pl.ds(part * (COLS // HALO_PARTS), COLS // HALO_PARTS)
        for side, rows in ((0, pl.ds(0, HALO)), (1, pl.ds(HALO + ROWS, HALO))):
            upper, lower = split(halo32[side, :, columns])
            high[rows, columns] = upper
            low[rows, columns] = lower
            halo2[side * HALO : (side + 1) * HALO, :] = upper
            halo2[(side + 2) * HALO : (side + 3) * HALO, :] = lower
        total = dot(halo2[...], spec2[:, columns], NT)
        total = total[: 2 * HALO] + total[2 * HALO :]
        acc[:HALO, :] += total[:HALO]
        acc[HALO + ROWS : PADDED, :] += total[HALO:]

    for s in range(SWEEPS):
        last_sweep = s == SWEEPS - 1
        for t in range(3):
            part = dot(acc[t * TILE : (t + 2) * TILE, :], warp[t], TN, HIGHEST)
            score_send[s, :, t * TILE : (t + 1) * TILE] = part[:K] + part[K:]
        copies = []
        for d in range(1, MZ_DEVS):
            j = lax.rem(mj + d, MZ_DEVS)
            rows = pl.ds(pl.multiple_of(j * 8, 8), 8)
            copies.append(send(score_send.at[s, rows], score_recv.at[s, d], mz=j))
        if s > 0:
            gram_copies = send_gram(s)
            settle(14)
        if s == 0:
            gram = unpack_gram(sum_slots(gram_recv.at[s], MZ_DEVS, gram_copies))
            inverse = factor_end(factor_steps(factor_start(gram), 0, 8))
        own = pl.ds(pl.multiple_of(mj * 8, 8), 8)
        total = score_send[s, own]
        for d in range(1, MZ_DEVS):
            copies[d - 1].wait_recv()
            total = total + score_recv[s, d]
        score_sum[s] = total
        score_all[s, own] = total
        copies = to_mz(score_sum.at[s], score_all.at[s, own])
        if s > 0:
            gram = unpack_gram(sum_slots(gram_recv.at[s], MZ_DEVS, gram_copies))
            eye = iota((K, K), 0) == iota((K, K), 1)
            diagonal = jnp.where(eye, gram, 0.0)
            down = 1.0 / jnp.sqrt(jnp.sum(diagonal, axis=1, keepdims=True) / MZ + rms_epsilon)
            across = 1.0 / jnp.sqrt(jnp.sum(diagonal, axis=0, keepdims=True) / MZ + rms_epsilon)
            gram = gram * down * across
            inverse = factor_end(factor_steps(factor_start(gram), 0, 8))
        for copy in copies:
            copy.wait_recv()
        scores = score_all[s]
        if s > 0:
            scores = scores * down
        conc = jnp.maximum(solve(inverse, scores), 0.0)
        if last_sweep:
            conc_out[...] = conc

        spread[...] = jnp.zeros_like(spread)
        for t in range(3):
            part = dot(conc[:, t * TILE : (t + 1) * TILE], warp[t], NT, HIGHEST)
            spread[:, t * TILE : (t + 2) * TILE] += part
        upper, lower = split(spread[...])
        spread2[:K] = upper
        spread2[K:] = lower

        packed = pack_gram(dot(conc, conc, NT, HIGHEST))
        conc_gram[s] = packed
        gram_copy = send(conc_gram.at[s], conc_gram_core.at[s], rows=partner)

        core_copies = {}
        y_copies = {}

        def cross_blocks(*several):
            for i in several:
                columns = block_columns(at_z(ORDER[i]))
                left = spread2[:, :PADDED]
                part = dot(left, high[:, columns], NN) + dot(left, low[:, columns], NN)
                part = part[:K] + part[K:]
                for c in range(2):
                    for h in range(2):
                        cross[s, i, c, h] = part[c * 32 : c * 32 + 32, h * HALF : h * HALF + HALF]
            for i in several:
                core_copies[i] = send(
                    cross.at[s, i, 1 - core], cross_core.at[s, i], rows=partner
                )

        def cross_add(i):
            core_copies[i].wait_recv()
            cross[s, i, core] += cross_core[s, i]

        def to_y(i):
            y_copies[i] = send(cross.at[s, i, core, 1 - y], cross_y.at[s, i], rows=y_pair)

        def y_sum(i):
            y_copies[i].wait_recv()
            return cross[s, i, core, y] + cross_y[s, i]

        cross_blocks(0, 1, 2)
        gram_copy.wait_recv()
        packed = conc_gram[s] + conc_gram_core[s]
        conc_gram_pair[s] = packed
        gram_copy = send(conc_gram_pair.at[s], conc_gram_y.at[s], rows=y_pair)
        cross_add(0)
        farther_copies = []
        for way in range(2):
            device = z_device(WAYS[way][1])
            farther_copies += [
                send(cross.at[s, 0, core, y, HALVES[way]], farther.at[s, way, 0], rows=device),
                send(
                    cross.at[s, 0, core, 1 - y, HALVES[way]],
                    farther.at[s, way, 1],
                    rows=other_plane(device),
                ),
            ]
        far_copies = []
        for way in range(2):
            cross_add(1 + way)
            device = z_device(WAYS[way][0])
            far_copies += [
                send(cross.at[s, 1 + way, core, y], far.at[s, way, 0], rows=device),
                send(
                    cross.at[s, 1 + way, core, 1 - y], far.at[s, way, 1], rows=other_plane(device)
                ),
            ]
        cross_blocks(3, 4)
        cross_blocks(5, 6)
        for i in (3, 4):
            cross_add(i)
            to_y(i)
        gram_copy.wait_recv()
        packed = conc_gram_pair[s] + conc_gram_y[s]
        conc_gram_total[...] = packed
        part = conc_gram_total[pl.ds(pl.multiple_of(16 * core, 16), 16)]
        conc_gram_all[s, z] = part
        gram_copies = to_z(conc_gram_all.at[s, z], conc_gram_all.at[s, z])
        cross_blocks(7)
        for i in (5, 6, 7):
            cross_add(i)
            to_y(i)
        settle(14)
        near_copies = []
        for way in range(2):
            total = y_sum(3 + way)
            for plane_copy in range(2):
                far_copies[2 * way + plane_copy].wait_recv()
                total = total + far[s, way, plane_copy]
            summed[s, 3 + way] = total
            for plane_copy in range(2):
                farther_copies[2 * way + plane_copy].wait_recv()
                summed[s, 3 + way, HALVES[way]] += farther[s, way, plane_copy]
            near_copies.append(
                send(summed.at[s, 3 + way], near.at[s, way], rows=z_device(WAYS[way][1]))
            )
        next_copies = []
        for way in range(2):
            summed[s, 5 + way] = y_sum(5 + way)
            next_copies.append(
                send(summed.at[s, 5 + way], next_to.at[s, way], rows=z_device(WAYS[way][0]))
            )
        conc_gram_sum[s, core] = sum_slots(conc_gram_all.at[s], RING, gram_copies)
        gram_copy = send(conc_gram_sum.at[s, core], conc_gram_sum.at[s, core], rows=partner)
        total = y_sum(7)
        gram_copy.wait_recv()
        groups = factor_steps(
            factor_start(unpack_gram(conc_gram_sum[s].reshape(K // 2, 2 * K))), 0, 4
        )
        for way in range(2):
            near_copies[way].wait_recv()
            total = total + near[s, way]
        for way in range(2):
            next_copies[way].wait_recv()
            total = total + next_to[s, way]
        owned[s, core] = total
        owned_copy = send(owned.at[s, core], owned.at[s, core], rows=partner)
        inverse = factor_end(factor_steps(groups, 4, 8))
        owned_copy.wait_recv()
        block = jnp.maximum(solve(inverse, owned[s].reshape(K, HALF)), 0.0)
        found[s, :, z, y] = block.reshape(2, K // 2, HALF)

        def pass_on(b, device, rows=None, planes=None):
            place = found.at[s, core, b, y if planes is None else planes]
            if rows is not None:
                place = place.at[rows]
            return send(place, place, rows=device)

        def to_core(b):
            place = found.at[s, core, b]
            return send(place, place, rows=partner)

        def use_blocks(*several):
            for b in several:
                for c in range(2):
                    for h in range(2):
                        first = pl.multiple_of(b * BLOCK + h * HALF, TILE)
                        columns = pl.ds(first, HALF)
                        rows = pl.ds(c * 32, 32)
                        if last_sweep:
                            store = pltpu.make_async_copy(
                                found.at[s, c, b, h],
                                spec_out.at[rows, columns],
                                store_sem.at[len(stores)],
                            )
                            store.start()
                            stores.append(store)
                        else:
                            upper, lower = split(found[s, c, b, h])
                            spec2[rows, columns] = upper
                            spec2[pl.ds(K + c * 32, 32), columns] = lower
            if not last_sweep:
                total = acc[:PADDED, :]
                for b in several:
                    columns = block_columns(b)
                    part = spec2[:, columns]
                    total = total + dot(high[:, columns], part, NT)
                    total = total + dot(low[:, columns], part, NT)
                acc[:PADDED, :] = total

        over_y = [pass_on(z, y_pair)]
        one_away = [pass_on(z, z_device(WAYS[way][0])) for way in range(2)]
        two_away = [pass_on(z, z_device(WAYS[way][1])) for way in range(2)]
        if last_sweep:
            x = block * block
            x = x[:, :TILE] + x[:, TILE : 2 * TILE] + x[:, 2 * TILE :]
            squares = dot(jnp.ones((8, TILE), F32), x, NT, HIGHEST)
            square_send[0] = squares
            square_mz[mj] = squares
            square_copies = to_mz(square_send.at[0], square_mz.at[mj])
        else:
            acc[...] = jnp.zeros_like(acc)
        ones = [at_z(RING - 1), at_z(1)]
        twos = [at_z(RING - 2), at_z(2)]
        threes = [at_z(RING - 3), at_z(3)]
        four = at_z(4)
        for way in range(2):
            one_away[way].wait_recv()
            over_y.append(pass_on(ones[way], y_pair))
        three_away, four_away = [], []
        for way in range(2):
            two_away[way].wait_recv()
            device = z_device(WAYS[way][0])
            three_away.append(pass_on(twos[way], device))
            device = z_device(WAYS[way][1])
            four_away.append(pass_on(twos[way], device, HALVES[way]))
            four_away.append(pass_on(twos[way], other_plane(device), HALVES[way]))
            over_y.append(pass_on(twos[way], y_pair))
        over_y[0].wait_recv()
        over_core = [pass_on(z, partner, planes=1 - y)]
        if last_sweep:
            squares = sum_slots(square_mz, MZ_DEVS, square_copies)
            square_z[z] = squares
            square_copies = to_z(square_z.at[z], square_z.at[z])
        for way in range(2):
            over_y[1 + way].wait_recv()
            over_core.append(to_core(ones[way]))
        over_core[0].wait_recv()
        use_blocks(z)
        for way in range(2):
            three_away[way].wait_recv()
            over_y.append(pass_on(threes[way], y_pair))
        for way in range(2):
            over_y[3 + way].wait_recv()
            over_core.append(to_core(twos[way]))
        for way in range(2):
            over_core[1 + way].wait_recv()
        use_blocks(*ones)
        for way in range(2):
            over_y[5 + way].wait_recv()
            over_core.append(to_core(threes[way]))
        if last_sweep:
            squares = sum_slots(square_z, RING, square_copies)
            square_send[1] = squares
            square_copy = send(square_send.at[1], square_y, rows=y_pair)
        for copy in four_away:
            copy.wait_recv()
        over_core.append(to_core(four))
        for way in range(2):
            over_core[3 + way].wait_recv()
        use_blocks(*twos)
        for way in range(2):
            over_core[5 + way].wait_recv()
        over_core[7].wait_recv()
        use_blocks(*threes, four)
        if last_sweep:
            settle(12)

    square_copy.wait_recv()
    across = 1.0 / jnp.sqrt((squares + square_y[...]) / MZ + rms_epsilon)
    scale_out[...] = across[0]
    for store in stores:
        store.wait()
    settle(0)


COPIES = 200


def body(raw_scans, scan_shift, scan_weight, spectra_init):
    any_space = pl.BlockSpec(memory_space=pl.ANY)
    vmem = pl.BlockSpec(memory_space=pltpu.VMEM)
    conc, spectra, scale = pl.pallas_call(
        kernel,
        out_shape=(
            jax.ShapeDtypeStruct((K, ROWS), F32),
            jax.ShapeDtypeStruct((K, COLS), F32),
            jax.ShapeDtypeStruct((K,), F32),
        ),
        in_specs=[any_space, vmem, vmem, any_space],
        out_specs=(vmem, any_space, vmem),
        scratch_shapes=[
            pltpu.VMEM((ROWS, COLS), F32),
            pltpu.VMEM((K, COLS), F32),
            pltpu.VMEM((2, HALO, COLS), F32),
            pltpu.VMEM((PADDED, COLS), BF16),
            pltpu.VMEM((PADDED, COLS), BF16),
            pltpu.VMEM((2 * K, COLS), BF16),
            pltpu.VMEM((4 * HALO, COLS // HALO_PARTS), BF16),
            pltpu.VMEM((3, 2 * TILE, TILE), F32),
            pltpu.VMEM((TALL, 2 * K), F32),
            pltpu.VMEM((SWEEPS, K // 2, 2 * K), F32),
            pltpu.VMEM((SWEEPS, MZ_DEVS, K // 2, 2 * K), F32),
            pltpu.VMEM((SWEEPS, K, ROWS), F32),
            pltpu.VMEM((SWEEPS, MZ_DEVS, 8, ROWS), F32),
            pltpu.VMEM((SWEEPS, 8, ROWS), F32),
            pltpu.VMEM((SWEEPS, K, ROWS), F32),
            pltpu.VMEM((SWEEPS, K // 2, 2 * K), F32),
            pltpu.VMEM((SWEEPS, K // 2, 2 * K), F32),
            pltpu.VMEM((SWEEPS, K // 2, 2 * K), F32),
            pltpu.VMEM((SWEEPS, K // 2, 2 * K), F32),
            pltpu.VMEM((SWEEPS, RING, K // 4, 2 * K), F32),
            pltpu.VMEM((SWEEPS, 2, K // 4, 2 * K), F32),
            pltpu.VMEM((K // 2, 2 * K), F32),
            pltpu.VMEM((K, TALL), F32),
            pltpu.VMEM((2 * K, TALL), BF16),
            pltpu.VMEM((SWEEPS, RING, 2, 2, K // 2, HALF), F32),
            pltpu.VMEM((SWEEPS, RING, 2, K // 2, HALF), F32),
            pltpu.VMEM((SWEEPS, RING, K // 2, HALF), F32),
            pltpu.VMEM((SWEEPS, 2, 2, K // 2, HALF), F32),
            pltpu.VMEM((SWEEPS, 2, 2, K // 4, HALF), F32),
            pltpu.VMEM((SWEEPS, 2, K // 2, HALF), F32),
            pltpu.VMEM((SWEEPS, 2, K // 2, HALF), F32),
            pltpu.VMEM((SWEEPS, RING, K // 2, HALF), F32),
            pltpu.VMEM((SWEEPS, 2, K // 2, HALF), F32),
            pltpu.VMEM((SWEEPS, 2, RING, 2, K // 2, HALF), F32),
            pltpu.VMEM((2, 8, K), F32),
            pltpu.VMEM((MZ_DEVS, 8, K), F32),
            pltpu.VMEM((RING, 8, K), F32),
            pltpu.VMEM((8, K), F32),
            pltpu.SemaphoreType.DMA((LOADS + 1,)),
            pltpu.SemaphoreType.DMA((4 * RING,)),
            pltpu.SemaphoreType.DMA((COPIES,)),
            pltpu.SemaphoreType.DMA((COPIES,)),
        ],
        compiler_params=pltpu.CompilerParams(
            collective_id=0, has_side_effects=True, vmem_limit_bytes=56 * 1024 * 1024
        ),
        name="mcr_als",
    )(raw_scans, scan_shift, scan_weight, spectra_init)
    return conc.T, spectra * scale[:, None]


def solution(mesh):
    return jax.shard_map(
        body,
        mesh=mesh,
        in_specs=(P("rows", "mz"), P("rows"), P("rows"), P(None, "mz")),
        out_specs=(P("rows", None), P(None, "mz")),
        check_vma=False,
    )
```

```python
import functools

import jax
import jax.numpy as jnp
from jax import lax
from jax.experimental import pallas as pl
from jax.experimental.pallas import tpu as pltpu
from jax.sharding import PartitionSpec as P

MESH = pl.DeviceIdType.MESH
F32 = jnp.float32
BF16 = jnp.bfloat16

MZ = 49152
K = 64
HALO = 16
SWEEPS = 2
ROW_DEVS = 32
MZ_DEVS = 8
RING = 8
ROWS = 384
PADDED = ROWS + 2 * HALO
TALL = 512
COLS = 6144
BLOCK = COLS // RING
HALF = BLOCK // 2
TILE = 128
HALO_PARTS = 2
LOADS = 4

fraction_unit = 256.0
rms_epsilon = 1e-06
ridge_share = 0.01

ORDER = (4, 3, 5, 2, 6, 1, 7, 0)
WAYS = ((1, 2), (7, 6))
HALVES = (pl.ds(0, K // 4), pl.ds(K // 4, K // 4))


def split(x):
    high = x.astype(BF16)
    return high, (x - high.astype(F32)).astype(BF16)


def dot(left, right, dims, precision=None):
    return lax.dot_general(
        left, right, (dims, ((), ())), precision=precision, preferred_element_type=F32
    )


NN = ((1,), (0,))
NT = ((1,), (1,))
TN = ((0,), (0,))
HIGHEST = lax.Precision.HIGHEST


def iota(shape, dim):
    return lax.broadcasted_iota(jnp.int32, shape, dim)


def pack_gram(gram):
    return jnp.concatenate([gram[: K // 2], gram[K // 2 :]], axis=1)


def unpack_gram(packed):
    return jnp.concatenate([packed[:, :K], packed[:, K:]], axis=0)


def factor_start(gram):
    eye = iota((K, K), 0) == iota((K, K), 1)
    diagonal = jnp.where(eye, gram, 0.0)
    trace = jnp.sum(jnp.sum(diagonal, axis=1, keepdims=True), axis=0, keepdims=True)
    ridge = ridge_share * trace / K
    unit = jnp.where(eye, 1.0, 0.0).astype(F32)
    joined = jnp.concatenate([gram + unit * ridge, unit], axis=1)
    return tuple(joined[8 * j : 8 * j + 8] for j in range(8))


def factor_steps(groups, first, last):
    sub = iota((8, 2 * K), 0)
    shape = (8, 2 * K)

    def step(g, groups):
        head = groups[0]
        columns = [jnp.broadcast_to(head[:, p : p + 1], shape) for p in range(8)]
        square = {}
        for p in range(8):
            for q in range(p, 8):
                square[q, p] = jnp.broadcast_to(columns[p][q : q + 1], shape)
        rows = [jnp.broadcast_to(head[p : p + 1], shape) for p in range(8)]
        inverse = []
        ratio = {}
        for p in range(8):
            inverse.append(1.0 / square[p, p])
            for q in range(p + 1, 8):
                ratio[q, p] = square[q, p] * inverse[p]
                for r in range(p + 1, q + 1):
                    square[q, r] = square[q, r] - ratio[q, p] * square[r, p]
                rows[q] = rows[q] - ratio[q, p] * rows[p]
        scaled = [rows[p] * inverse[p] for p in range(8)]
        done = rows[0]
        for p in range(8):
            root = lax.rsqrt(square[p, p])
            root = root * (1.5 - 0.5 * square[p, p] * root * root)
            done = jnp.where(sub == p, rows[p] * root, done)
        rest = []
        for j in range(1, 8):
            left = [groups[j][:, p : p + 1] for p in range(8)]
            left = [jnp.broadcast_to(x, shape) for x in left]
            for p in range(7):
                for q in range(p + 1, 8):
                    left[q] = left[q] - ratio[q, p] * left[p]
            terms = [left[p] * scaled[p] for p in range(8)]
            while len(terms) > 1:
                terms = [terms[i] + terms[i + 1] for i in range(0, len(terms), 2)]
            rest.append(groups[j] - jnp.where(j < 8 - g, terms[0], 0.0))
        return tuple(pltpu.roll(x, 2 * K - 8, 1) for x in rest + [done])

    return lax.fori_loop(first, last, step, groups)


def factor_end(groups):
    return jnp.concatenate(groups, axis=0)[:, :K]


def solve(inverse_factor, target):
    return dot(inverse_factor, dot(inverse_factor, target, NN, HIGHEST), TN, HIGHEST)


def kernel(
    raw, shift, weight, spec, conc_out, spec_out, scale_out,
    raw32, spec32, halo32, high, low, spec2, halo2, warp, acc,
    gram_send, gram_recv, score_send, score_recv, score_sum, score_all,
    conc_gram, conc_gram_core, conc_gram_pair, conc_gram_y, conc_gram_all, conc_gram_sum, conc_gram_total,
    spread, spread2, cross, cross_core, cross_y, far, farther, near, next_to, summed, owned,
    found, square_send, square_mz, square_z, square_y, load_sem, store_sem, send_sem, recv_sem,
):
    ri = lax.axis_index("rows")
    mj = lax.axis_index("mz")
    core = lax.rem(ri, 2)
    z = lax.rem(lax.div(ri, 2), RING)
    plane = ri - 2 * z

    def at_z(distance):
        return lax.rem(z + distance, RING)

    def z_device(distance):
        return plane + 2 * at_z(distance)

    def other_plane(device):
        return lax.rem(device + 16, ROW_DEVS)

    partner = ri + 1 - 2 * core
    y = lax.div(ri, 16)
    y_pair = lax.rem(ri + 16, ROW_DEVS)
    row_next = lax.rem(ri + 1, ROW_DEVS)
    row_back = lax.rem(ri + ROW_DEVS - 1, ROW_DEVS)
    started = []
    settled = []
    stores = []

    def send(source, target, rows=None, mz=None):
        number = len(started)
        copy = pltpu.make_async_remote_copy(
            src_ref=source,
            dst_ref=target,
            send_sem=send_sem.at[number],
            recv_sem=recv_sem.at[number],
            device_id=(ri if rows is None else rows, mj if mz is None else mz),
            device_id_type=MESH,
        )
        copy.start()
        started.append(copy)
        return copy

    def settle(keep):
        while len(settled) < len(started) - keep:
            started[len(settled)].wait_send()
            settled.append(True)

    def to_mz(source, target):
        return [
            send(source, target, mz=lax.rem(mj + d, MZ_DEVS)) for d in range(1, MZ_DEVS)
        ]

    def to_z(source, target):
        return [send(source, target, rows=z_device(d)) for d in range(1, RING)]

    def sum_slots(slots, count, copies):
        for copy in copies:
            copy.wait_recv()
        total = slots[0]
        for j in range(1, count):
            total = total + slots[j]
        return total

    def block_columns(b):
        return pl.ds(pl.multiple_of(b * BLOCK, TILE), BLOCK)

    spec_load = pltpu.make_async_copy(spec, spec32, load_sem.at[LOADS])
    spec_load.start()
    loads = []
    for b in range(LOADS):
        columns = pl.ds(b * (COLS // LOADS), COLS // LOADS)
        loads.append(pltpu.make_async_copy(raw.at[:, columns], raw32.at[:, columns], load_sem.at[b]))
        loads[-1].start()

    barrier = pltpu.get_barrier_semaphore()
    peers = [(ri, lax.rem(mj + d, MZ_DEVS)) for d in range(1, MZ_DEVS)]
    peers += [(z_device(d), mj) for d in range(1, RING)]
    peers += [(other_plane(z_device(d)), mj) for d in (1, 2, 6, 7)]
    peers += [(y_pair, mj), (row_next, mj), (row_back, mj)]
    for peer in peers:
        pl.semaphore_signal(barrier, inc=1, device_id=peer, device_id_type=MESH)

    pl.semaphore_wait(barrier, len(peers))
    halos = []
    for part in range(HALO_PARTS):
        columns = pl.ds(part * (COLS // HALO_PARTS), COLS // HALO_PARTS)
        halos.append((
            send(raw.at[pl.ds(ROWS - HALO, HALO), columns], halo32.at[0, :, columns], rows=row_next),
            send(raw.at[pl.ds(0, HALO), columns], halo32.at[1, :, columns], rows=row_back),
        ))

    for t in range(3):
        tile = pl.ds(t * TILE, TILE)
        target = iota((2 * TILE, TILE), 1) + shift[tile].reshape(1, TILE) + HALO
        fraction = weight[tile].reshape(1, TILE).astype(F32) / fraction_unit
        row = iota((2 * TILE, TILE), 0)
        warp[t] = jnp.where(row == target, 1.0 - fraction, 0.0) + jnp.where(
            row == target + 1, fraction, 0.0
        )
    acc[...] = jnp.zeros_like(acc)

    def send_gram(s):
        total = dot(spec2[...], spec2[...], NT)
        total = total[:K] + total[K:]
        packed = pack_gram(total[:, :K] + total[:, K:])
        gram_send[s] = packed
        gram_recv[s, mj] = packed
        return to_mz(gram_send.at[s], gram_recv.at[s, mj])

    spec_load.wait()

    def first_spectra(b, carry):
        columns = block_columns(b)
        upper, lower = split(spec32[:, columns])
        spec2[:K, columns] = upper
        spec2[K:, columns] = lower
        return carry

    lax.fori_loop(0, RING, first_spectra, 0)

    gram_copies = send_gram(0)

    for b in range(LOADS):
        loads[b].wait()
        columns = pl.ds(b * (COLS // LOADS), COLS // LOADS)

        def split_rows(r, carry):
            rows = pl.multiple_of(r * HALO, HALO)
            upper, lower = split(raw32[pl.ds(rows, HALO), columns])
            rows = pl.multiple_of(rows + HALO, HALO)
            high[pl.ds(rows, HALO), columns] = upper
            low[pl.ds(rows, HALO), columns] = lower
            return carry

        lax.fori_loop(0, ROWS // 16, split_rows, 0)
        part = spec2[:, columns]
        own = pl.ds(HALO, ROWS)
        acc[own, :] += dot(high[own, columns], part, NT) + dot(low[own, columns], part, NT)

    for part in range(HALO_PARTS):
        for copy in halos[part]:
            copy.wait_recv()
        columns = pl.ds(part * (COLS // HALO_PARTS), COLS // HALO_PARTS)
        for side, rows in ((0, pl.ds(0, HALO)), (1, pl.ds(HALO + ROWS, HALO))):
            upper, lower = split(halo32[side, :, columns])
            high[rows, columns] = upper
            low[rows, columns] = lower
            halo2[side * HALO : (side + 1) * HALO, :] = upper
            halo2[(side + 2) * HALO : (side + 3) * HALO, :] = lower
        total = dot(halo2[...], spec2[:, columns], NT)
        total = total[: 2 * HALO] + total[2 * HALO :]
        acc[:HALO, :] += total[:HALO]
        acc[HALO + ROWS : PADDED, :] += total[HALO:]

    for s in range(SWEEPS):
        last_sweep = s == SWEEPS - 1
        for t in range(3):
            part = dot(acc[t * TILE : (t + 2) * TILE, :], warp[t], TN, HIGHEST)
            score_send[s, :, t * TILE : (t + 1) * TILE] = part[:K] + part[K:]
        copies = []
        for d in range(1, MZ_DEVS):
            j = lax.rem(mj + d, MZ_DEVS)
            rows = pl.ds(pl.multiple_of(j * 8, 8), 8)
            copies.append(send(score_send.at[s, rows], score_recv.at[s, d], mz=j))
        if s > 0:
            gram_copies = send_gram(s)
            settle(14)
        if s == 0:
            gram = unpack_gram(sum_slots(gram_recv.at[s], MZ_DEVS, gram_copies))
            inverse = factor_end(factor_steps(factor_start(gram), 0, 8))
        own = pl.ds(pl.multiple_of(mj * 8, 8), 8)
        total = score_send[s, own]
        for d in range(1, MZ_DEVS):
            copies[d - 1].wait_recv()
            total = total + score_recv[s, d]
        score_sum[s] = total
        score_all[s, own] = total
        copies = to_mz(score_sum.at[s], score_all.at[s, own])
        if s > 0:
            gram = unpack_gram(sum_slots(gram_recv.at[s], MZ_DEVS, gram_copies))
            eye = iota((K, K), 0) == iota((K, K), 1)
            diagonal = jnp.where(eye, gram, 0.0)
            down = 1.0 / jnp.sqrt(jnp.sum(diagonal, axis=1, keepdims=True) / MZ + rms_epsilon)
            across = 1.0 / jnp.sqrt(jnp.sum(diagonal, axis=0, keepdims=True) / MZ + rms_epsilon)
            gram = gram * down * across
            inverse = factor_end(factor_steps(factor_start(gram), 0, 8))
        for copy in copies:
            copy.wait_recv()
        scores = score_all[s]
        if s > 0:
            scores = scores * down
        conc = jnp.maximum(solve(inverse, scores), 0.0)
        if last_sweep:
            conc_out[...] = conc

        spread[...] = jnp.zeros_like(spread)
        for t in range(3):
            part = dot(conc[:, t * TILE : (t + 1) * TILE], warp[t], NT, HIGHEST)
            spread[:, t * TILE : (t + 2) * TILE] += part
        upper, lower = split(spread[...])
        spread2[:K] = upper
        spread2[K:] = lower

        packed = pack_gram(dot(conc, conc, NT, HIGHEST))
        conc_gram[s] = packed
        gram_copy = send(conc_gram.at[s], conc_gram_core.at[s], rows=partner)

        core_copies = {}
        y_copies = {}

        def cross_blocks(*several):
            for i in several:
                columns = block_columns(at_z(ORDER[i]))
                left = spread2[:, :PADDED]
                part = dot(left, high[:, columns], NN) + dot(left, low[:, columns], NN)
                part = part[:K] + part[K:]
                for c in range(2):
                    for h in range(2):
                        cross[s, i, c, h] = part[c * 32 : c * 32 + 32, h * HALF : h * HALF + HALF]
            for i in several:
                core_copies[i] = send(
                    cross.at[s, i, 1 - core], cross_core.at[s, i], rows=partner
                )

        def cross_add(i):
            core_copies[i].wait_recv()
            cross[s, i, core] += cross_core[s, i]

        def to_y(i):
            y_copies[i] = send(cross.at[s, i, core, 1 - y], cross_y.at[s, i], rows=y_pair)

        def y_sum(i):
            y_copies[i].wait_recv()
            return cross[s, i, core, y] + cross_y[s, i]

        cross_blocks(0, 1, 2)
        gram_copy.wait_recv()
        packed = conc_gram[s] + conc_gram_core[s]
        conc_gram_pair[s] = packed
        gram_copy = send(conc_gram_pair.at[s], conc_gram_y.at[s], rows=y_pair)
        cross_add(0)
        farther_copies = []
        for way in range(2):
            device = z_device(WAYS[way][1])
            farther_copies += [
                send(cross.at[s, 0, core, y, HALVES[way]], farther.at[s, way, 0], rows=device),
                send(
                    cross.at[s, 0, core, 1 - y, HALVES[way]],
                    farther.at[s, way, 1],
                    rows=other_plane(device),
                ),
            ]
        for i in (1, 2):
            cross_add(i)
            to_y(i)
        cross_blocks(3, 4)
        cross_blocks(5, 6)
        for i in (3, 4):
            cross_add(i)
            to_y(i)
        gram_copy.wait_recv()
        packed = conc_gram_pair[s] + conc_gram_y[s]
        conc_gram_total[...] = packed
        part = conc_gram_total[pl.ds(pl.multiple_of(16 * core, 16), 16)]
        conc_gram_all[s, z] = part
        gram_copies = to_z(conc_gram_all.at[s, z], conc_gram_all.at[s, z])
        far_copies = []
        for way in range(2):
            summed[s, 1 + way] = y_sum(1 + way)
            far_copies.append(
                send(summed.at[s, 1 + way], far.at[s, way], rows=z_device(WAYS[way][0]))
            )
        cross_blocks(7)
        for i in (5, 6, 7):
            cross_add(i)
            to_y(i)
        settle(14)
        near_copies = []
        for way in range(2):
            total = y_sum(3 + way)
            far_copies[way].wait_recv()
            total = total + far[s, way]
            summed[s, 3 + way] = total
            for plane_copy in range(2):
                farther_copies[2 * way + plane_copy].wait_recv()
                summed[s, 3 + way, HALVES[way]] += farther[s, way, plane_copy]
            near_copies.append(
                send(summed.at[s, 3 + way], near.at[s, way], rows=z_device(WAYS[way][1]))
            )
        next_copies = []
        for way in range(2):
            summed[s, 5 + way] = y_sum(5 + way)
            next_copies.append(
                send(summed.at[s, 5 + way], next_to.at[s, way], rows=z_device(WAYS[way][0]))
            )
        conc_gram_sum[s, core] = sum_slots(conc_gram_all.at[s], RING, gram_copies)
        gram_copy = send(conc_gram_sum.at[s, core], conc_gram_sum.at[s, core], rows=partner)
        total = y_sum(7)
        gram_copy.wait_recv()
        groups = factor_steps(
            factor_start(unpack_gram(conc_gram_sum[s].reshape(K // 2, 2 * K))), 0, 4
        )
        for way in range(2):
            near_copies[way].wait_recv()
            total = total + near[s, way]
        for way in range(2):
            next_copies[way].wait_recv()
            total = total + next_to[s, way]
        owned[s, core] = total
        owned_copy = send(owned.at[s, core], owned.at[s, core], rows=partner)
        inverse = factor_end(factor_steps(groups, 4, 8))
        owned_copy.wait_recv()
        block = jnp.maximum(solve(inverse, owned[s].reshape(K, HALF)), 0.0)
        found[s, :, z, y] = block.reshape(2, K // 2, HALF)

        def pass_on(b, device, rows=None, planes=None):
            place = found.at[s, core, b, y if planes is None else planes]
            if rows is not None:
                place = place.at[rows]
            return send(place, place, rows=device)

        def to_core(b):
            place = found.at[s, core, b]
            return send(place, place, rows=partner)

        def use_blocks(*several):
            for b in several:
                for c in range(2):
                    for h in range(2):
                        first = pl.multiple_of(b * BLOCK + h * HALF, TILE)
                        columns = pl.ds(first, HALF)
                        rows = pl.ds(c * 32, 32)
                        if last_sweep:
                            store = pltpu.make_async_copy(
                                found.at[s, c, b, h],
                                spec_out.at[rows, columns],
                                store_sem.at[len(stores)],
                            )
                            store.start()
                            stores.append(store)
                        else:
                            upper, lower = split(found[s, c, b, h])
                            spec2[rows, columns] = upper
                            spec2[pl.ds(K + c * 32, 32), columns] = lower
            if not last_sweep:
                total = acc[:PADDED, :]
                for b in several:
                    columns = block_columns(b)
                    part = spec2[:, columns]
                    total = total + dot(high[:, columns], part, NT)
                    total = total + dot(low[:, columns], part, NT)
                acc[:PADDED, :] = total

        over_y = [pass_on(z, y_pair)]
        one_away = [pass_on(z, z_device(WAYS[way][0])) for way in range(2)]
        two_away = [pass_on(z, z_device(WAYS[way][1])) for way in range(2)]
        if last_sweep:
            x = block * block
            x = x[:, :TILE] + x[:, TILE : 2 * TILE] + x[:, 2 * TILE :]
            squares = dot(jnp.ones((8, TILE), F32), x, NT, HIGHEST)
            square_send[0] = squares
            square_mz[mj] = squares
            square_copies = to_mz(square_send.at[0], square_mz.at[mj])
        else:
            acc[...] = jnp.zeros_like(acc)
        ones = [at_z(RING - 1), at_z(1)]
        twos = [at_z(RING - 2), at_z(2)]
        threes = [at_z(RING - 3), at_z(3)]
        four = at_z(4)
        for way in range(2):
            one_away[way].wait_recv()
            over_y.append(pass_on(ones[way], y_pair))
        three_away, four_away = [], []
        for way in range(2):
            two_away[way].wait_recv()
            device = z_device(WAYS[way][0])
            three_away.append(pass_on(twos[way], device))
            device = z_device(WAYS[way][1])
            four_away.append(pass_on(twos[way], device, HALVES[way]))
            four_away.append(pass_on(twos[way], other_plane(device), HALVES[way]))
            over_y.append(pass_on(twos[way], y_pair))
        over_y[0].wait_recv()
        over_core = [pass_on(z, partner, planes=1 - y)]
        if last_sweep:
            squares = sum_slots(square_mz, MZ_DEVS, square_copies)
            square_z[z] = squares
            square_copies = to_z(square_z.at[z], square_z.at[z])
        for way in range(2):
            over_y[1 + way].wait_recv()
            over_core.append(to_core(ones[way]))
        over_core[0].wait_recv()
        use_blocks(z)
        for way in range(2):
            three_away[way].wait_recv()
            over_y.append(pass_on(threes[way], y_pair))
        for way in range(2):
            over_y[3 + way].wait_recv()
            over_core.append(to_core(twos[way]))
        for way in range(2):
            over_core[1 + way].wait_recv()
        use_blocks(*ones)
        for way in range(2):
            over_y[5 + way].wait_recv()
            over_core.append(to_core(threes[way]))
        if last_sweep:
            squares = sum_slots(square_z, RING, square_copies)
            square_send[1] = squares
            square_copy = send(square_send.at[1], square_y, rows=y_pair)
        for copy in four_away:
            copy.wait_recv()
        over_core.append(to_core(four))
        for way in range(2):
            over_core[3 + way].wait_recv()
        use_blocks(*twos)
        for way in range(2):
            over_core[5 + way].wait_recv()
        over_core[7].wait_recv()
        use_blocks(*threes, four)
        if last_sweep:
            settle(12)

    square_copy.wait_recv()
    across = 1.0 / jnp.sqrt((squares + square_y[...]) / MZ + rms_epsilon)
    scale_out[...] = across[0]
    for store in stores:
        store.wait()
    settle(0)


COPIES = 200


def body(raw_scans, scan_shift, scan_weight, spectra_init):
    any_space = pl.BlockSpec(memory_space=pl.ANY)
    vmem = pl.BlockSpec(memory_space=pltpu.VMEM)
    conc, spectra, scale = pl.pallas_call(
        kernel,
        out_shape=(
            jax.ShapeDtypeStruct((K, ROWS), F32),
            jax.ShapeDtypeStruct((K, COLS), F32),
            jax.ShapeDtypeStruct((K,), F32),
        ),
        in_specs=[any_space, vmem, vmem, any_space],
        out_specs=(vmem, any_space, vmem),
        scratch_shapes=[
            pltpu.VMEM((ROWS, COLS), F32),
            pltpu.VMEM((K, COLS), F32),
            pltpu.VMEM((2, HALO, COLS), F32),
            pltpu.VMEM((PADDED, COLS), BF16),
            pltpu.VMEM((PADDED, COLS), BF16),
            pltpu.VMEM((2 * K, COLS), BF16),
            pltpu.VMEM((4 * HALO, COLS // HALO_PARTS), BF16),
            pltpu.VMEM((3, 2 * TILE, TILE), F32),
            pltpu.VMEM((TALL, 2 * K), F32),
            pltpu.VMEM((SWEEPS, K // 2, 2 * K), F32),
            pltpu.VMEM((SWEEPS, MZ_DEVS, K // 2, 2 * K), F32),
            pltpu.VMEM((SWEEPS, K, ROWS), F32),
            pltpu.VMEM((SWEEPS, MZ_DEVS, 8, ROWS), F32),
            pltpu.VMEM((SWEEPS, 8, ROWS), F32),
            pltpu.VMEM((SWEEPS, K, ROWS), F32),
            pltpu.VMEM((SWEEPS, K // 2, 2 * K), F32),
            pltpu.VMEM((SWEEPS, K // 2, 2 * K), F32),
            pltpu.VMEM((SWEEPS, K // 2, 2 * K), F32),
            pltpu.VMEM((SWEEPS, K // 2, 2 * K), F32),
            pltpu.VMEM((SWEEPS, RING, K // 4, 2 * K), F32),
            pltpu.VMEM((SWEEPS, 2, K // 4, 2 * K), F32),
            pltpu.VMEM((K // 2, 2 * K), F32),
            pltpu.VMEM((K, TALL), F32),
            pltpu.VMEM((2 * K, TALL), BF16),
            pltpu.VMEM((SWEEPS, RING, 2, 2, K // 2, HALF), F32),
            pltpu.VMEM((SWEEPS, RING, 2, K // 2, HALF), F32),
            pltpu.VMEM((SWEEPS, RING, K // 2, HALF), F32),
            pltpu.VMEM((SWEEPS, 2, K // 2, HALF), F32),
            pltpu.VMEM((SWEEPS, 2, 2, K // 4, HALF), F32),
            pltpu.VMEM((SWEEPS, 2, K // 2, HALF), F32),
            pltpu.VMEM((SWEEPS, 2, K // 2, HALF), F32),
            pltpu.VMEM((SWEEPS, RING, K // 2, HALF), F32),
            pltpu.VMEM((SWEEPS, 2, K // 2, HALF), F32),
            pltpu.VMEM((SWEEPS, 2, RING, 2, K // 2, HALF), F32),
            pltpu.VMEM((2, 8, K), F32),
            pltpu.VMEM((MZ_DEVS, 8, K), F32),
            pltpu.VMEM((RING, 8, K), F32),
            pltpu.VMEM((8, K), F32),
            pltpu.SemaphoreType.DMA((LOADS + 1,)),
            pltpu.SemaphoreType.DMA((4 * RING,)),
            pltpu.SemaphoreType.DMA((COPIES,)),
            pltpu.SemaphoreType.DMA((COPIES,)),
        ],
        compiler_params=pltpu.CompilerParams(
            collective_id=0, has_side_effects=True, vmem_limit_bytes=56 * 1024 * 1024
        ),
        name="mcr_als",
    )(raw_scans, scan_shift, scan_weight, spectra_init)
    return conc.T, spectra * scale[:, None]


def solution(mesh):
    return jax.shard_map(
        body,
        mesh=mesh,
        in_specs=(P("rows", "mz"), P("rows"), P("rows"), P(None, "mz")),
        out_specs=(P("rows", None), P(None, "mz")),
        check_vma=False,
    )
```
